512 devices in a mesh: seq: 128 (over y, x, z_lo, core), tp: 4 (over z_hi).
Axes of the slice: x: 4, y: 8, z: 8 (z_hi: 4, z_lo: 2; z = z_hi * 2 + z_lo), core: 2. Of those that a mesh axis runs over, the one named last changes fastest.
Arguments:
- tokens: bfloat16 [16384, 2048], P('seq', 'tp'), may hold values from -6 to 6
- norm_gain: float32 [2048], replicated, may hold values from 0.25 to 1.75
- in_weight: bfloat16 [2048, 3, 2048], P('seq', None, 'tp'), may hold values from -0.125 to 0.125
- short_taps: float32 [3, 3, 2048], P(None, None, 'tp'), may hold values from -3.5 to 3.5
- filter_response: float32 [16384, 2048], P('seq', 'tp'), may hold values from -1.1 to 1.1
- skip_gain: float32 [2048], P('tp'), may hold values from -4 to 4
- out_weight: bfloat16 [2048, 2048], P('seq', 'tp'), may hold values from -0.125 to 0.125
Outputs:
- hyena_out: bfloat16 [16384, 2048], P('seq', 'tp')
The draws below stay inside these ranges and needn't reach their ends.
All inputs are finite; a program needn't handle non-finite values.
Results may differ from the reference program's by a relative error of at most 0.017.
Values may be sent and summed in bfloat16 or wider, within the bound.
No kernel may reach another device: no remote copies, remote signals or barrier semaphores. Data moves between devices by JAX's collectives and lax.ppermute only.
A program may use at most 64 MiB of HBM per device.

```python
import math
import jax
import jax.numpy as jnp
from jax import lax

D = 2048
SHORT = 3
TOKENS = 16384


def draw_filter_response(key, part):
    key = jax.random.fold_in(key, 3)
    key_kind, key_slow, key_fast, key_noise = jax.random.split(key, 4)
    slow_share = 0.5
    slow_flag = jax.random.uniform(key_kind, (1, D), jnp.float32) < slow_share
    slow_rate = jnp.exp(jax.random.uniform(key_slow, (1, D), jnp.float32, minval=jnp.log(0.25), maxval=jnp.log(0.75))) / TOKENS
    fast_rate = jnp.exp(jax.random.uniform(key_fast, (1, D), jnp.float32, minval=jnp.log(1.0 / 50.0), maxval=jnp.log(1.0 / 30.0)))
    positions = jnp.arange(TOKENS, dtype=jnp.int32).astype(jnp.float32)[:, None]
    slow_part = jnp.exp(-slow_rate * positions) * jnp.sqrt(2.0 * slow_rate)
    fast_part = 0.9 * jnp.exp(-fast_rate * positions) * jnp.sqrt(2.0 * fast_rate)
    envelope = slow_part + jnp.where(slow_flag, 0.0, fast_part)
    noise = jnp.clip(jax.random.normal(key_noise, (TOKENS, D), jnp.float32), -4.0, 4.0)
    return jnp.clip(noise * envelope, -1.1, 1.1)


def block_scale(rng, dims, shards, least, high):
    def one(dim, parts):
        draws = jax.random.uniform(jax.random.fold_in(jax.random.fold_in(rng, 6), dim), (parts,), jnp.float32, least / len(shards), high / len(shards))
        return jnp.repeat(jnp.exp(draws), dims[dim] // parts).reshape((-1,) + (1,) * (len(dims) - dim - 1))

    level = one(*shards[0])
    for cut in shards[1:]:
        level = level * one(*cut)
    return level


def bell_draw(key, dims, scale, reach, shards=(), held_as=jnp.bfloat16):
    gain = block_scale(key, dims, shards, -0.22, 0.18) if shards else 1.0
    entries = jax.random.normal(key, dims, jnp.float32) * scale * gain
    return jnp.minimum(jnp.maximum(entries, -reach), reach).astype(held_as)


def setup_inputs(seed: int = 0) -> dict:
    arg_keys = jax.random.split(jax.random.key(seed), 8)
    return {
        "tokens": bell_draw(arg_keys[0], (TOKENS, D), 1.0, 6.0, ((0, 128), (1, 4))),
        "norm_gain": jnp.clip(1.0 + 0.15 * jax.random.normal(arg_keys[1], (D,), jnp.float32), 0.25, 1.75),
        "in_weight": bell_draw(arg_keys[2], (D, 3, D), D ** -0.5, 0.125, ((0, 128), (2, 4))),
        "short_taps": bell_draw(arg_keys[3], (SHORT, 3, D), SHORT ** -0.5, 3.5, ((2, 4),), jnp.float32),
        "filter_response": draw_filter_response(jax.random.fold_in(arg_keys[7], 71), 0),
        "skip_gain": bell_draw(arg_keys[5], (D,), 1.0, 4.0, ((0, 4),), jnp.float32),
        "out_weight": bell_draw(arg_keys[6], (D, D), D ** -0.5, 0.125, ((0, 128), (1, 4))),
    }


def convolve_block(block_pair):
    signal_block, filter_block = block_pair
    seq_length = signal_block.shape[0]
    fft_length = 2 * seq_length
    spectrum = jnp.fft.rfft(signal_block, n=fft_length, axis=0) * jnp.fft.rfft(filter_block, n=fft_length, axis=0)
    return jnp.fft.irfft(spectrum, n=fft_length, axis=0)[:seq_length]

def reference(tokens, norm_gain, in_weight, short_taps, filter_response, skip_gain, out_weight):
    features = tokens.astype(jnp.float32)
    mean_square = lax.optimization_barrier(jnp.mean(features * features, axis=1, keepdims=True))
    normed = (features * lax.rsqrt(mean_square + 1e-05) * norm_gain).astype(jnp.bfloat16)
    summed = jnp.dot(normed, in_weight.reshape(D, 3 * D), preferred_element_type=jnp.float32)
    projected = summed.reshape(TOKENS, 3, D).astype(jnp.bfloat16)
    padded = jnp.concatenate([jnp.zeros((2, 3, D), jnp.bfloat16), projected], axis=0).astype(jnp.float32)
    shortconv = short_taps[0] * padded[2:] + short_taps[1] * padded[1:TOKENS + 1] + short_taps[2] * padded[:TOKENS]
    query_part = shortconv[:, 0]
    signal = shortconv[:, 1] * shortconv[:, 2]
    width_block = math.gcd(D, 128)
    groups = D // width_block
    signal_blocks = signal.reshape(TOKENS, groups, width_block).transpose(1, 0, 2)
    filter_blocks = filter_response.reshape(TOKENS, groups, width_block).transpose(1, 0, 2)
    convolved = lax.map(convolve_block, (signal_blocks, filter_blocks))
    convolved = convolved.transpose(1, 0, 2).reshape(TOKENS, D)
    mixed_sum = convolved + skip_gain * signal
    gated_rows = (query_part * mixed_sum).astype(jnp.bfloat16)
    return jnp.dot(gated_rows, out_weight, preferred_element_type=jnp.float32).astype(jnp.bfloat16)
```

```python
import functools
import math

import jax
import jax.numpy as jnp
import numpy as np
from jax import lax
from jax.experimental import pallas as pl
from jax.experimental.pallas import tpu as pltpu
from jax.sharding import Mesh
from jax.sharding import PartitionSpec as P

F32 = jnp.float32
BF16 = jnp.bfloat16
LANES = 128
HALO = 16
OUTER = ("y", "x")
INNER = ("zl", "co")
SEQ = OUTER + INNER


def call(body, out_shape, *args, limit=48):
    return pl.pallas_call(
        body,
        out_shape=out_shape,
        compiler_params=pltpu.CompilerParams(vmem_limit_bytes=limit * 1024 * 1024),
    )(*args)


def transform_tables(length, chans, outer, inner):
    blocks = length // LANES
    row = np.arange(blocks)
    lane = np.arange(LANES)
    far = np.exp(-2j * np.pi * (row[:, None] * (4 * row[None, :] + 1) % (4 * blocks)) / (4 * blocks))
    near = np.exp(-2j * np.pi * (lane[:, None] * lane[None, :] % LANES) / LANES)
    turn = np.exp(-2j * np.pi * ((4 * row[:, None] + 1) * lane[None, :] % (4 * length)) / (4 * length))
    eye = np.eye(chans)
    into = np.einsum("bf,cd->cfbd", far, eye).reshape(chans * blocks, blocks * chans)
    into = np.concatenate([into.real, into.imag], axis=0)
    back = np.einsum("bf,cd->bdcf", far.conj(), eye).reshape(blocks * chans, chans * blocks) / length
    back = np.concatenate([back.real, -back.imag], axis=1)
    near_in = np.block([[near.real, near.imag], [-near.imag, near.real]])
    near_out = np.block([[near.real, -near.imag], [near.imag, near.real]])
    turn = np.stack([np.tile(turn.real, (chans, 1)), np.tile(turn.imag, (chans, 1))])
    as_short = lambda table: jnp.asarray(table.astype(np.float32)).astype(BF16)
    return {
        "into": as_short(into),
        "back": as_short(back),
        "near_in": as_short(near_in),
        "near_out": as_short(near_out),
        "turn": jnp.asarray(turn.astype(np.float32)),
    }


def forward_points(block, into, near_in, turn):
    half = into.shape[0] // 2
    far = jnp.dot(into, block, preferred_element_type=F32)
    real, imag = far[:half], far[half:]
    cos, sin = turn[0], turn[1]
    pair = jnp.concatenate([real * cos - imag * sin, real * sin + imag * cos], axis=1)
    return jnp.dot(pair.astype(BF16), near_in, preferred_element_type=F32)


def filter_body(taps_ref, into_ref, near_ref, turn_ref, out_ref):
    out_ref[...] = forward_points(taps_ref[...], into_ref[...], near_ref[...], turn_ref[...])


def conv_body(sig_ref, spec_ref, into_ref, near_in_ref, turn_ref, near_out_ref, back_ref, out_ref):
    groups, rows, lanes = sig_ref.shape
    block = sig_ref[...].reshape(groups * rows, lanes)
    turn = turn_ref[...]
    points = forward_points(block, into_ref[...], near_in_ref[...], turn)
    spec = spec_ref[...]
    real, imag = points[:, :lanes], points[:, lanes:]
    sreal, simag = spec[:, :lanes], spec[:, lanes:]
    pair = jnp.concatenate([real * sreal - imag * simag, real * simag + imag * sreal], axis=1)
    near = jnp.dot(pair.astype(BF16), near_out_ref[...], preferred_element_type=F32)
    real, imag = near[:, :lanes], near[:, lanes:]
    cos, sin = turn[0], turn[1]
    stacked = jnp.concatenate([real * cos + imag * sin, imag * cos - real * sin], axis=0)
    result = jnp.dot(back_ref[...], stacked.astype(BF16), preferred_element_type=F32)
    out_ref[...] = result.astype(BF16).reshape(groups, rows, lanes)


def norm_body(tok_ref, halo_ref, gain_ref, out_ref):
    inner, tp, length, feats = tok_ref.shape
    width = tp * feats

    def put(parts, at, rows):
        total = sum(jnp.sum(part * part, axis=1, keepdims=True) for part in parts)
        scale = lax.rsqrt(total / width + 1e-05)
        for p, part in enumerate(parts):
            gain = gain_ref[:, p * feats : (p + 1) * feats]
            out_ref[at : at + rows, p * feats : (p + 1) * feats] = (part * scale * gain).astype(BF16)

    put([halo_ref[p].astype(F32) for p in range(tp)], 0, HALO)
    for s in range(inner):
        put([tok_ref[s, p].astype(F32) for p in range(tp)], HALO + s * length, length)


def project_body(x_ref, w_ref, taps_ref, query_ref, signal_ref, send_ref):
    _, parts, _, chans = w_ref.shape
    depth = x_ref.shape[1]
    groups, rows, lanes = send_ref.shape
    inner = query_ref.shape[0] // lanes
    per = rows // inner
    weight = jnp.concatenate([w_ref[:, s].reshape(depth, chans) for s in range(parts)], axis=1)
    proj = jnp.dot(x_ref[...], weight, preferred_element_type=F32).astype(BF16).astype(F32)
    short = taps_ref[0:1] * proj
    for lag in range(1, taps_ref.shape[0]):
        short = short + taps_ref[lag : lag + 1] * pltpu.roll(proj, lag, 0)
    short = short[HALO:]
    query_ref[...] = short[:, :chans]
    signal = short[:, chans : 2 * chans] * short[:, 2 * chans :]
    signal_ref[...] = signal
    pieces = [signal[b * lanes : (b + 1) * lanes].T.reshape(groups, per, lanes) for b in range(inner)]
    send_ref[...] = jnp.concatenate(pieces, axis=1).astype(BF16)


def gate_body(conv_ref, query_ref, signal_ref, skip_ref, out_ref):
    groups, rows, lanes = conv_ref.shape
    inner = query_ref.shape[0] // lanes
    per = rows // inner
    conv = conv_ref[...].astype(F32)
    for b in range(inner):
        piece = conv[:, b * per : (b + 1) * per].reshape(groups * per, lanes).T
        at = slice(b * lanes, (b + 1) * lanes)
        mixed = piece + skip_ref[...] * signal_ref[at]
        out_ref[at] = (query_ref[at] * mixed).astype(BF16)


def out_body(gated_ref, w_ref, out_ref):
    inner, tp, rows, chans = gated_ref.shape
    x = jnp.concatenate([gated_ref[s, p] for p in range(tp) for s in range(inner)], axis=1)
    out_ref[...] = jnp.dot(x, w_ref[...], preferred_element_type=F32).astype(BF16)


def shape(dims, dtype):
    return jax.ShapeDtypeStruct(dims, dtype)


def shards(ways, tables, tokens, norm_gain, in_weight, short_taps, filter_response, skip_gain, out_weight):
    outer = ways["y"] * ways["x"]
    inner = ways["zl"] * ways["co"]
    tp = ways["tp"]
    length, feats = tokens.shape
    chans = skip_gain.shape[0] // inner
    per = chans // outer
    depth, parts = in_weight.shape[0], in_weight.shape[1]
    rows = inner * per
    place = lax.axis_index(INNER)

    with jax.named_scope("weight_gather"):
        split = in_weight.reshape(depth, parts, inner, chans).transpose(2, 1, 0, 3)
        swapped = lax.all_to_all(split, INNER, 0, 0)
        weight = lax.all_gather(swapped, OUTER, axis=0)
        weight = weight.reshape(outer * inner, parts, depth, chans)
    with jax.named_scope("token_gather"):
        tok = lax.all_gather(tokens, INNER + ("tp",), axis=0).reshape(inner, tp, length, feats)
        halo = lax.ppermute(
            tok[inner - 1, :, length - HALO :], OUTER, [(i, i + 1) for i in range(outer - 1)]
        )
    with jax.named_scope("filter_points"):
        taps = filter_response.astype(BF16).T.reshape(inner, outer, per, length)
        taps = taps.transpose(1, 0, 2, 3).reshape(outer * inner, per, length)
        taps = lax.all_to_all(taps, SEQ, 0, 0).reshape(outer * inner * per, length)
        spec = call(
            filter_body,
            shape((per * outer * inner, 2 * LANES), F32),
            taps,
            tables["into"],
            tables["near_in"],
            tables["turn"],
        )
    with jax.named_scope("out_weight_gather"):
        out_w = lax.all_to_all(
            jnp.broadcast_to(out_weight[None], (outer * inner,) + out_weight.shape), SEQ, 0, 0
        ).reshape(outer * inner * out_weight.shape[0], out_weight.shape[1])
    with jax.named_scope("norm"):
        x = call(
            norm_body,
            shape((HALO + inner * length, tp * feats), BF16),
            tok,
            halo,
            norm_gain.reshape(1, tp * feats),
        )
    with jax.named_scope("project"):
        own_taps = lax.dynamic_slice_in_dim(short_taps, place * chans, chans, 2)
        query, signal, send = call(
            project_body,
            (
                shape((inner * length, chans), F32),
                shape((inner * length, chans), F32),
                shape((outer, rows, LANES), BF16),
            ),
            x,
            weight,
            own_taps.reshape(short_taps.shape[0], parts * chans),
        )
    with jax.named_scope("conv"):
        blocks = lax.all_to_all(send, OUTER, 0, 0)
        conv = call(
            conv_body,
            shape((outer, rows, LANES), BF16),
            blocks,
            spec,
            tables["into"],
            tables["near_in"],
            tables["turn"],
            tables["near_out"],
            tables["back"],
        )
        conv = lax.all_to_all(conv, OUTER, 0, 0)
    with jax.named_scope("gate"):
        own_skip = lax.dynamic_slice_in_dim(skip_gain, place * chans, chans, 0)
        gated = call(
            gate_body,
            shape((inner * length, chans), BF16),
            conv,
            query,
            signal,
            own_skip.reshape(1, chans),
        )
    with jax.named_scope("gated_gather"):
        gated = jnp.broadcast_to(
            gated.reshape(inner, 1, length, chans), (inner, tp, length, chans)
        ).reshape(inner * tp, length, chans)
        gated = lax.all_to_all(gated, INNER + ("tp",), 0, 0).reshape(inner, tp, length, chans)
    with jax.named_scope("out_project"):
        return call(out_body, shape((length, out_w.shape[1]), BF16), gated, out_w)


def solution(mesh):
    seq, tp = mesh.shape["seq"], mesh.shape["tp"]
    ways = {"y": seq // 16, "x": 4, "zl": 2, "co": 2, "tp": tp}
    fine = Mesh(mesh.devices.reshape(tuple(ways.values())), tuple(ways))
    placed = (
        P(SEQ, "tp"),
        P(),
        P(SEQ, None, "tp"),
        P(None, None, "tp"),
        P(SEQ, "tp"),
        P("tp"),
        P(SEQ, "tp"),
    )

    def run(*args):
        tokens, skip = args[0], args[5]
        inner = ways["zl"] * ways["co"]
        per = skip.shape[0] // (tp * seq)
        tables = transform_tables(tokens.shape[0], per, seq // inner, inner)
        body = functools.partial(shards, ways, tables)
        return jax.shard_map(
            body, mesh=fine, in_specs=placed, out_specs=P(SEQ, "tp"), check_vma=False
        )(*args)

    return run
```

```python
import functools
import math

import jax
import jax.numpy as jnp
import numpy as np
from jax import lax
from jax.experimental import pallas as pl
from jax.experimental.pallas import tpu as pltpu
from jax.sharding import Mesh
from jax.sharding import PartitionSpec as P

F32 = jnp.float32
BF16 = jnp.bfloat16
LANES = 128
HALO = 16
OUTER = ("y", "x")
INNER = ("zl", "co")
SEQ = OUTER + INNER


def call(body, out_shape, *args, scalars=0, scratch=()):
    specs = [pl.BlockSpec(memory_space=pltpu.SMEM)] * scalars
    specs += [pl.BlockSpec(memory_space=pltpu.VMEM)] * (len(args) - scalars)
    return pl.pallas_call(
        body,
        out_shape=out_shape,
        in_specs=specs,
        scratch_shapes=scratch,
        compiler_params=pltpu.CompilerParams(vmem_limit_bytes=20 * 1024 * 1024),
    )(*args)


def transform_tables(length, chans, outer, inner):
    blocks = length // LANES
    row = np.arange(blocks)
    lane = np.arange(LANES)
    far = np.exp(-2j * np.pi * (row[:, None] * (4 * row[None, :] + 1) % (4 * blocks)) / (4 * blocks))
    near = np.exp(-2j * np.pi * (lane[:, None] * lane[None, :] % LANES) / LANES)
    turn = np.exp(-2j * np.pi * ((4 * row[:, None] + 1) * lane[None, :] % (4 * length)) / (4 * length))
    eye = np.eye(chans)
    into = np.einsum("bf,cd->cfbd", far, eye).reshape(chans * blocks, blocks * chans)
    into = np.concatenate([into.real, into.imag], axis=0)
    back = np.einsum("bf,cd->bdcf", far.conj(), eye).reshape(blocks * chans, chans * blocks) / length
    back = np.concatenate([back.real, -back.imag], axis=1)
    near_in = np.block([[near.real, near.imag], [-near.imag, near.real]])
    near_out = np.block([[near.real, -near.imag], [near.imag, near.real]])
    turn = np.stack([np.tile(turn.real, (chans, 1)), np.tile(turn.imag, (chans, 1))])
    as_short = lambda table: jnp.asarray(table.astype(np.float32)).astype(BF16)
    return {
        "into": as_short(into),
        "back": as_short(back),
        "near_in": as_short(near_in),
        "near_out": as_short(near_out),
        "turn": jnp.asarray(turn.astype(np.float32)),
    }


def forward_points(block, into, near_in, turn):
    half = into.shape[0] // 2
    far = jnp.dot(into, block, preferred_element_type=F32)
    real, imag = far[:half], far[half:]
    cos, sin = turn[0], turn[1]
    pair = jnp.concatenate([real * cos - imag * sin, real * sin + imag * cos], axis=1)
    return jnp.dot(pair.astype(BF16), near_in, preferred_element_type=F32)


def filter_body(taps_ref, into_ref, near_ref, turn_ref, out_ref):
    out_ref[...] = forward_points(taps_ref[...], into_ref[...], near_ref[...], turn_ref[...])


def conv_body(sig_ref, spec_ref, into_ref, near_in_ref, turn_ref, near_out_ref, back_ref, out_ref):
    groups, rows, lanes = sig_ref.shape
    block = sig_ref[...].reshape(groups * rows, lanes)
    turn = turn_ref[...]
    points = forward_points(block, into_ref[...], near_in_ref[...], turn)
    spec = spec_ref[...]
    real, imag = points[:, :lanes], points[:, lanes:]
    sreal, simag = spec[:, :lanes], spec[:, lanes:]
    pair = jnp.concatenate([real * sreal - imag * simag, real * simag + imag * sreal], axis=1)
    near = jnp.dot(pair.astype(BF16), near_out_ref[...], preferred_element_type=F32)
    real, imag = near[:, :lanes], near[:, lanes:]
    cos, sin = turn[0], turn[1]
    stacked = jnp.concatenate([real * cos + imag * sin, imag * cos - real * sin], axis=0)
    result = jnp.dot(back_ref[...], stacked.astype(BF16), preferred_element_type=F32)
    out_ref[...] = result.astype(BF16).reshape(groups, rows, lanes)


def pack_body(weight_ref, out_w_ref, taps_ref, send_ref):
    parts = weight_ref.shape[0]
    lanes = send_ref.shape[3]
    inner = out_w_ref.shape[1] // lanes
    ways = send_ref.shape[0] // inner
    rows = send_ref.shape[2]
    for s in range(inner):
        at = slice(s * lanes, (s + 1) * lanes)
        taps = taps_ref[:, at].T.reshape(ways, rows, lanes).astype(BF16)
        for way in range(ways):
            to = way * inner + s
            for part in range(parts):
                send_ref[to, part] = weight_ref[part, :, at]
            send_ref[to, parts] = out_w_ref[:, at]
            send_ref[to, parts + 1] = taps[way]


def repack_body(got_ref, send_ref):
    sources, kinds, rows, lanes = got_ref.shape
    ways, tiles = send_ref.shape[0], send_ref.shape[1]
    parts = kinds - 1
    taps = got_ref[:, parts].astype(F32)
    per = rows // ways
    for way in range(ways):
        for part in range(parts):
            send_ref[way, part * sources : (part + 1) * sources] = got_ref[:, part]
        piece = taps[:, way * per : (way + 1) * per].reshape(tiles - parts * sources, rows, lanes)
        send_ref[way, parts * sources :] = piece.astype(BF16)


def scaled(parts, gain_ref):
    width = gain_ref.shape[1]
    total = sum(jnp.sum(part * part, axis=1, keepdims=True) for part in parts)
    scale = lax.rsqrt(total / width + 1e-05)
    feats = width // len(parts)
    return [
        (part * scale * gain_ref[:, p * feats : (p + 1) * feats]).astype(BF16)
        for p, part in enumerate(parts)
    ]


def norm_body(tok_ref, gain_ref, out_ref):
    count, length, feats = tok_ref.shape
    tp = out_ref.shape[1] // feats
    for block in range(count // tp):
        parts = [tok_ref[block * tp + p].astype(F32) for p in range(tp)]
        for p, part in enumerate(scaled(parts, gain_ref)):
            out_ref[block * length : (block + 1) * length, p * feats : (p + 1) * feats] = part


def project_body(
    cores,
    core_ref,
    own_ref,
    other_ref,
    halo_own_ref,
    halo_other_ref,
    gain_ref,
    got_ref,
    taps_ref,
    query_ref,
    signal_ref,
    send_ref,
    out_w_ref,
    filter_ref,
    proj_ref,
):
    core = core_ref[0, 0]
    parts = 3
    ways, tiles, rows, lanes = got_ref.shape
    groups = send_ref.shape[0]
    outer = groups // ways
    inner = query_ref.shape[0] // lanes
    chans = query_ref.shape[1]
    per = send_ref.shape[1] // inner
    sources = outer * inner

    def column(part):
        pieces = [
            got_ref[x, part * sources + y * inner : part * sources + (y + 1) * inner].reshape(
                inner * rows, lanes
            )
            for y in range(outer)
            for x in range(ways)
        ]
        return jnp.concatenate(pieces, axis=0)

    weight = jnp.concatenate([column(part) for part in range(parts)], axis=1)
    out_w_ref[...] = column(parts)
    first = (parts + 1) * sources
    for y in range(outer):
        for x in range(ways):
            at = (y * ways + x) * rows
            filter_ref[at : at + rows] = got_ref[x, first + y]

    def project(block):
        got = jnp.dot(block, weight, preferred_element_type=F32)
        return got.astype(BF16).astype(F32)

    halo = jnp.where(core == cores - 1, halo_own_ref[...].astype(F32), halo_other_ref[...].astype(F32))
    halo = scaled([halo[p] for p in range(halo.shape[0])], gain_ref)
    proj_ref[:HALO] = project(jnp.concatenate(halo, axis=1))
    for ref, at_core in ((own_ref, core), (other_ref, 1 - core)):
        got = project(ref[...])
        for z in range(inner // cores):
            at = pl.multiple_of(HALO + (z * cores + at_core) * lanes, HALO)
            proj_ref[pl.ds(at, lanes)] = got[z * lanes : (z + 1) * lanes]

    count = query_ref.shape[0]
    short = taps_ref[0:1] * proj_ref[HALO:]
    for lag in range(1, taps_ref.shape[0]):
        short = short + taps_ref[lag : lag + 1] * proj_ref[HALO - lag : HALO - lag + count]
    query_ref[...] = short[:, :chans]
    signal = short[:, chans : 2 * chans] * short[:, 2 * chans :]
    signal_ref[...] = signal
    pieces = [signal[b * lanes : (b + 1) * lanes].T.reshape(groups, per, lanes) for b in range(inner)]
    send_ref[...] = jnp.concatenate(pieces, axis=1).astype(BF16)


def gate_body(conv_ref, query_ref, signal_ref, skip_ref, out_ref):
    groups, rows, lanes = conv_ref.shape
    inner = query_ref.shape[0] // lanes
    per = rows // inner
    conv = conv_ref[...].astype(F32)
    for b in range(inner):
        piece = conv[:, b * per : (b + 1) * per].reshape(groups * per, lanes).T
        at = slice(b * lanes, (b + 1) * lanes)
        mixed = piece + skip_ref[...] * signal_ref[at]
        gated = (query_ref[at] * mixed).astype(BF16)
        for p in range(out_ref.shape[1]):
            out_ref[b, p] = gated


def out_body(place_ref, gated_ref, own_ref, near_ref, across_ref, out_ref):
    place = place_ref[0, 0]
    inner, tp, rows, chans = gated_ref.shape
    x = jnp.concatenate([gated_ref[s, p] for p in range(tp) for s in range(inner)], axis=1)
    weight = jnp.concatenate([own_ref[...], near_ref[...], across_ref[0], across_ref[1]], axis=1)
    out = jnp.dot(x, weight, preferred_element_type=F32).astype(BF16)
    for k, flip in enumerate((0, 2, 1, 3)):
        at = pl.multiple_of((place ^ flip) * chans, chans)
        out_ref[:, pl.ds(at, chans)] = out[:, k * chans : (k + 1) * chans]


def shape(dims, dtype):
    return jax.ShapeDtypeStruct(dims, dtype)


def swap(value, axis):
    return lax.ppermute(value, axis, [(0, 1), (1, 0)])


def shards(ways, tables, tokens, norm_gain, in_weight, short_taps, filter_response, skip_gain, out_weight):
    outer = ways["y"] * ways["x"]
    cores = ways["co"]
    inner = ways["zl"] * cores
    tp = ways["tp"]
    length, feats = tokens.shape
    chans = skip_gain.shape[0] // inner
    per = chans // outer
    depth, parts = in_weight.shape[0], in_weight.shape[1]
    rows = inner * per
    place = lax.axis_index(INNER)
    core = lax.axis_index("co")
    as_scalar = lambda value: value.astype(jnp.int32).reshape(1, 1)
    gain = norm_gain.reshape(1, tp * feats)

    with jax.named_scope("token_gather"):
        own = lax.all_gather(tokens, ("zl", "tp"), axis=0)
        other = swap(own, "co")
        tail = own[own.shape[0] - tp :, length - HALO :]
        halo_own = lax.ppermute(tail, OUTER, [(i, i + 1) for i in range(outer - 1)])
        halo_other = lax.ppermute(
            tail,
            OUTER + ("co",),
            [(i * cores + cores - 1, (i + 1) * cores) for i in range(outer - 1)],
        )
    with jax.named_scope("weight_gather"):
        kinds = parts + 2
        send = call(
            pack_body,
            shape((ways["y"] * inner, kinds, depth, LANES), BF16),
            in_weight.transpose(1, 0, 2),
            out_weight,
            filter_response,
        )
        got = lax.all_to_all(send, ("y",) + INNER, 0, 0)
        tiles = (kinds - 1) * ways["y"] * inner + ways["y"] * inner // ways["x"]
        send = call(repack_body, shape((ways["x"], tiles, depth, LANES), BF16), got)
        got = lax.all_to_all(send, "x", 0, 0)
    with jax.named_scope("norm"):
        normed = shape((ways["zl"] * length, tp * feats), BF16)
        x_own = call(norm_body, normed, own, gain)
        x_other = call(norm_body, normed, other, gain)
    with jax.named_scope("project"):
        own_taps = lax.dynamic_slice_in_dim(short_taps, place * chans, chans, 2)
        query, signal, send, out_w, taps = call(
            functools.partial(project_body, cores),
            (
                shape((inner * length, chans), F32),
                shape((inner * length, chans), F32),
                shape((outer, rows, LANES), BF16),
                shape((outer * inner * depth, chans), BF16),
                shape((outer * rows, LANES), BF16),
            ),
            as_scalar(core),
            x_own,
            x_other,
            halo_own,
            halo_other,
            gain,
            got,
            own_taps.reshape(short_taps.shape[0], parts * chans),
            scalars=1,
            scratch=[pltpu.VMEM((HALO + inner * length, parts * chans), F32)],
        )
    with jax.named_scope("conv"):
        blocks = lax.all_to_all(send, OUTER, 0, 0)
        spec = call(
            filter_body,
            shape((per * outer * inner, 2 * LANES), F32),
            taps,
            tables["into"],
            tables["near_in"],
            tables["turn"],
        )
        conv = call(
            conv_body,
            shape((outer, rows, LANES), BF16),
            blocks,
            spec,
            tables["into"],
            tables["near_in"],
            tables["turn"],
            tables["near_out"],
            tables["back"],
        )
        conv = lax.all_to_all(conv, OUTER, 0, 0)
    with jax.named_scope("out_weight_swap"):
        near_w = swap(out_w, "zl")
        across_w = swap(jnp.stack([out_w, near_w]), "co")
    with jax.named_scope("gate"):
        own_skip = lax.dynamic_slice_in_dim(skip_gain, place * chans, chans, 0)
        gated = call(
            gate_body,
            shape((inner, tp, length, chans), BF16),
            conv,
            query,
            signal,
            own_skip.reshape(1, chans),
        )
        gated = lax.all_to_all(
            gated.reshape(inner * tp, length, chans), INNER + ("tp",), 0, 0
        ).reshape(inner, tp, length, chans)
    with jax.named_scope("out_project"):
        return call(
            out_body,
            shape((length, out_weight.shape[1]), BF16),
            as_scalar(place),
            gated,
            out_w,
            near_w,
            across_w,
            scalars=1,
        )


def solution(mesh):
    seq, tp = mesh.shape["seq"], mesh.shape["tp"]
    ways = {"y": seq // 16, "x": 4, "zl": 2, "co": 2, "tp": tp}
    fine = Mesh(mesh.devices.reshape(tuple(ways.values())), tuple(ways))
    placed = (
        P(SEQ, "tp"),
        P(),
        P(SEQ, None, "tp"),
        P(None, None, "tp"),
        P(SEQ, "tp"),
        P("tp"),
        P(SEQ, "tp"),
    )

    def run(*args):
        tokens, skip = args[0], args[5]
        inner = ways["zl"] * ways["co"]
        per = skip.shape[0] // (tp * seq)
        tables = transform_tables(tokens.shape[0], per, seq // inner, inner)
        body = functools.partial(shards, ways, tables)
        return jax.shard_map(
            body, mesh=fine, in_specs=placed, out_specs=P(SEQ, "tp"), check_vma=False
        )(*args)

    return run
```

```python
import functools
import math

import jax
import jax.numpy as jnp
import numpy as np
from jax import lax
from jax.experimental import pallas as pl
from jax.experimental.pallas import tpu as pltpu
from jax.sharding import Mesh
from jax.sharding import PartitionSpec as P

F32 = jnp.float32
BF16 = jnp.bfloat16
LANES = 128
HALO = 16
KERNEL_VMEM = 60 * 1024 * 1024
OUTER = ("y", "x")
INNER = ("zl", "co")
SEQ = OUTER + INNER


def call(body, out_shape, places, args, scratch=()):
    spaces = {"h": pltpu.HBM, "v": pltpu.VMEM, "s": pltpu.SMEM}
    specs = [pl.BlockSpec(memory_space=spaces[place]) for place in places]
    single = not isinstance(out_shape, tuple)
    outs = specs[len(args) :]
    return pl.pallas_call(
        body,
        out_shape=out_shape,
        in_specs=specs[: len(args)],
        out_specs=outs[0] if single else tuple(outs),
        scratch_shapes=scratch,
        compiler_params=pltpu.CompilerParams(vmem_limit_bytes=KERNEL_VMEM),
    )(*args)


def started(pairs, sems, first=0):
    copies = [
        pltpu.make_async_copy(source, target, sems.at[first + k])
        for k, (source, target) in enumerate(pairs)
    ]
    for copy in copies:
        copy.start()
    return copies


def finish(copies):
    for copy in copies:
        copy.wait()


def transform_tables(length, chans, outer, inner):
    blocks = length // LANES
    row = np.arange(blocks)
    lane = np.arange(LANES)
    far = np.exp(-2j * np.pi * (row[:, None] * (4 * row[None, :] + 1) % (4 * blocks)) / (4 * blocks))
    near = np.exp(-2j * np.pi * (lane[:, None] * lane[None, :] % LANES) / LANES)
    turn = np.exp(-2j * np.pi * ((4 * row[:, None] + 1) * lane[None, :] % (4 * length)) / (4 * length))
    eye = np.eye(chans)
    into = np.einsum("bf,cd->cfbd", far, eye).reshape(chans * blocks, blocks * chans)
    into = np.concatenate([into.real, into.imag], axis=0)
    back = np.einsum("bf,cd->bdcf", far.conj(), eye).reshape(blocks * chans, chans * blocks) / length
    back = np.concatenate([back.real, -back.imag], axis=1)
    near_in = np.block([[near.real, near.imag], [-near.imag, near.real]])
    near_out = np.block([[near.real, -near.imag], [near.imag, near.real]])
    turn = np.stack([turn.real, turn.imag])
    as_short = lambda table: jnp.asarray(table.astype(np.float32)).astype(BF16)
    return {
        "into": as_short(into),
        "back": as_short(back),
        "near_in": as_short(near_in),
        "near_out": as_short(near_out),
        "turn": jnp.asarray(turn.astype(np.float32)),
    }


def times(real, imag, cos, sin):
    return real * cos - imag * sin, real * sin + imag * cos


def turned(pair, turn_ref, sign, axis):
    chans = pair[0].shape[0] // turn_ref.shape[1]
    cos = jnp.concatenate([turn_ref[0]] * chans, axis=0)
    sin = jnp.concatenate([turn_ref[1]] * chans, axis=0) * sign
    return jnp.concatenate(times(*pair, cos, sin), axis=axis).astype(BF16)


def halves(value, axis):
    half = value.shape[axis] // 2
    return lax.slice_in_dim(value, 0, half, axis=axis), lax.slice_in_dim(value, half, 2 * half, axis=axis)


def filter_body(got_ref, into_hbm, near_hbm, turn_hbm, out_hbm, into_ref, near_ref, turn_ref, out_ref, sems):
    copies = started([(into_hbm, into_ref), (turn_hbm, turn_ref), (near_hbm, near_ref)], sems)
    ways, outer = got_ref.shape[:2]
    block = jnp.concatenate([got_ref[x, y] for y in range(outer) for x in range(ways)], axis=0)
    copies[0].wait()
    far = jnp.dot(into_ref[...], block, preferred_element_type=F32)
    copies[1].wait()
    pair = turned(halves(far, 0), turn_ref, 1.0, 1)
    copies[2].wait()
    out_ref[...] = jnp.dot(pair, near_ref[...], preferred_element_type=F32)
    finish(started([(out_ref, out_hbm)], sems, len(copies)))


def conv_body(
    sig_ref,
    spec_hbm,
    into_hbm,
    near_in_hbm,
    turn_hbm,
    near_out_hbm,
    back_hbm,
    out_hbm,
    spec_ref,
    into_ref,
    near_in_ref,
    turn_ref,
    near_out_ref,
    back_ref,
    out_ref,
    sems,
):
    copies = started(
        [
            (into_hbm, into_ref),
            (turn_hbm, turn_ref),
            (near_in_hbm, near_in_ref),
            (spec_hbm, spec_ref),
            (near_out_hbm, near_out_ref),
            (back_hbm, back_ref),
        ],
        sems,
    )
    groups, rows, lanes = sig_ref.shape
    block = sig_ref[...].reshape(groups * rows, lanes)
    copies[0].wait()
    far = jnp.dot(into_ref[...], block, preferred_element_type=F32)
    copies[1].wait()
    pair = turned(halves(far, 0), turn_ref, 1.0, 1)
    copies[2].wait()
    points = jnp.dot(pair, near_in_ref[...], preferred_element_type=F32)
    copies[3].wait()
    product = times(*halves(points, 1), *halves(spec_ref[...], 1))
    pair = jnp.concatenate(product, axis=1).astype(BF16)
    copies[4].wait()
    near = jnp.dot(pair, near_out_ref[...], preferred_element_type=F32)
    pair = turned(halves(near, 1), turn_ref, -1.0, 0)
    copies[5].wait()
    result = jnp.dot(back_ref[...], pair, preferred_element_type=F32)
    out_ref[...] = result.astype(BF16).reshape(groups, rows, lanes)
    finish(started([(out_ref, out_hbm)], sems, len(copies)))


def pack_body(weight_hbm, out_w_hbm, taps_hbm, send_hbm, weight_ref, out_w_ref, taps_ref, send_ref, sems):
    copies = started([(taps_hbm, taps_ref), (weight_hbm, weight_ref), (out_w_hbm, out_w_ref)], sems)
    parts = weight_ref.shape[0]
    total, _, rows, lanes = send_ref.shape
    inner = out_w_ref.shape[1] // lanes
    ways = total // inner
    copies[0].wait()
    for s in range(inner):
        taps = taps_ref[:, s * lanes : (s + 1) * lanes].T.reshape(ways, rows, lanes).astype(BF16)
        for way in range(ways):
            send_ref[way * inner + s, parts + 1] = taps[way]
    finish(copies[1:])
    for s in range(inner):
        at = slice(s * lanes, (s + 1) * lanes)
        for way in range(ways):
            for part in range(parts):
                send_ref[way * inner + s, part] = weight_ref[part, :, at]
            send_ref[way * inner + s, parts] = out_w_ref[:, at]
    finish(started([(send_ref, send_hbm)], sems, len(copies)))


def repack_body(got_ref, weight_hbm, taps_hbm, taps_ref, sems):
    kinds, rows, lanes = got_ref.shape[1:]
    parts = kinds - 1
    copies = started([(got_ref.at[:, :parts], weight_hbm)], sems)
    ways, outer = taps_ref.shape[:2]
    taps = got_ref[:, parts].astype(F32)
    per = rows // ways
    for way in range(ways):
        piece = taps[:, way * per : (way + 1) * per].reshape(outer, rows, lanes)
        taps_ref[way] = piece.astype(BF16)
    finish(copies + started([(taps_ref, taps_hbm)], sems, len(copies)))


def project_body(
    cores,
    place_ref,
    own_hbm,
    other_hbm,
    halo_own_hbm,
    halo_other_hbm,
    gain_ref,
    taps_ref,
    here_hbm,
    before_hbm,
    after_hbm,
    across_low_hbm,
    across_high_hbm,
    spec_hbm,
    query_hbm,
    signal_hbm,
    send_hbm,
    out_w_hbm,
    tok_ref,
    halo_ref,
    x_ref,
    w_ref,
    proj_ref,
    query_ref,
    signal_ref,
    send_ref,
    sems,
):
    core, x = place_ref[0, 0], place_ref[0, 1]
    tokens = started(
        [
            (own_hbm, tok_ref.at[0]),
            (other_hbm, tok_ref.at[1]),
            (halo_own_hbm, halo_ref.at[0]),
            (halo_other_hbm, halo_ref.at[1]),
        ],
        sems,
    )
    parts, outer, ways = w_ref.shape[0], w_ref.shape[1], w_ref.shape[2]
    half = outer // 2
    pairs = []
    for source, step, low, count in (
        (here_hbm, 0, 0, outer),
        (before_hbm, ways - 1, 0, outer),
        (after_hbm, 1, 0, outer),
        (across_low_hbm, 2, 0, half),
        (across_high_hbm, 2, half, half),
    ):
        to = lax.rem(x + step, ways)
        for part in range(parts):
            pairs.append((source.at[:, :, part], w_ref.at[part, pl.ds(low, count), to]))
        pairs.append((source.at[:, :, parts], out_w_hbm.at[pl.ds(low, count), to]))
    weights = started(pairs, sems, len(tokens))

    _, blocks, length, feats = tok_ref.shape
    tp = x_ref.shape[1] // feats
    inner = (x_ref.shape[0] - HALO) // length

    def put(pieces, at):
        total = sum(jnp.sum(piece * piece, axis=1, keepdims=True) for piece in pieces)
        scale = lax.rsqrt(total / (tp * feats) + 1e-05)
        for p, piece in enumerate(pieces):
            gain = gain_ref[:, p * feats : (p + 1) * feats]
            x_ref[at, p * feats : (p + 1) * feats] = (piece * scale * gain).astype(BF16)

    zs = inner // cores
    for side in range(2):
        tokens[side].wait()
        at_core = core if side == 0 else cores - 1 - core
        for z in range(zs):
            at = pl.multiple_of(HALO + (z * cores + at_core) * length, HALO)
            put([tok_ref[side, p * zs + z].astype(F32) for p in range(tp)], pl.ds(at, length))
    finish(tokens[2:])
    put(
        [
            jnp.where(core == cores - 1, halo_ref[0, p].astype(F32), halo_ref[1, p].astype(F32))
            for p in range(tp)
        ],
        slice(0, HALO),
    )
    finish(weights)
    depth = x_ref.shape[1]
    chans = query_ref.shape[1]
    weight = jnp.concatenate([w_ref[part].reshape(depth, chans) for part in range(parts)], axis=1)
    proj = jnp.dot(x_ref[...], weight, preferred_element_type=F32)
    proj_ref[...] = proj.astype(BF16).astype(F32)

    count = query_ref.shape[0]
    short = taps_ref[0:1] * proj_ref[HALO:]
    for lag in range(1, taps_ref.shape[0]):
        short = short + taps_ref[lag : lag + 1] * proj_ref[HALO - lag : HALO - lag + count]
    signal = short[:, chans : 2 * chans] * short[:, 2 * chans :]
    groups, rows, lanes = send_ref.shape
    pieces = [
        signal[b * lanes : (b + 1) * lanes].T.reshape(groups, rows // inner, lanes) for b in range(inner)
    ]
    send_ref[...] = jnp.concatenate(pieces, axis=1).astype(BF16)
    first = len(tokens) + len(weights)
    copies = started([(send_ref, send_hbm)], sems, first)
    query_ref[...] = short[:, :chans]
    signal_ref[...] = signal
    copies += started([(query_ref, query_hbm), (signal_ref, signal_hbm)], sems, first + 1)
    finish(copies)


def gate_body(conv_ref, query_hbm, signal_hbm, skip_ref, out_ref, query_ref, signal_ref, sems):
    copies = started([(query_hbm, query_ref), (signal_hbm, signal_ref)], sems)
    groups, rows, lanes = conv_ref.shape
    inner = query_ref.shape[0] // lanes
    per = rows // inner
    conv = conv_ref[...].astype(F32)
    pieces = [conv[:, b * per : (b + 1) * per].reshape(groups * per, lanes).T for b in range(inner)]
    finish(copies)
    for b, piece in enumerate(pieces):
        at = slice(b * lanes, (b + 1) * lanes)
        mixed = piece + skip_ref[...] * signal_ref[at]
        gated = (query_ref[at] * mixed).astype(BF16)
        for p in range(out_ref.shape[1]):
            out_ref[b, p] = gated


def out_body(gated_ref, w_hbm, out_ref, w_ref, sems):
    inner, tp, rows, chans = gated_ref.shape
    copies = started([(w_hbm.at[s], w_ref.at[s]) for s in range(inner)], sems)
    x = jnp.concatenate([gated_ref[s, p] for p in range(tp) for s in range(inner)], axis=1)
    finish(copies)
    weight = jnp.concatenate([w_ref[s] for s in range(inner)], axis=1)
    out_ref[...] = jnp.dot(x, weight, preferred_element_type=F32).astype(BF16)


def shape(dims, dtype):
    return jax.ShapeDtypeStruct(dims, dtype)


def swap(value, axis):
    return lax.ppermute(value, axis, [(0, 1), (1, 0)])


def ring(value, axis, count, step):
    return lax.ppermute(value, axis, [(i, (i + step) % count) for i in range(count)])


def held(*arrays):
    return [pltpu.VMEM(array.shape, array.dtype) for array in arrays]


def copies_of(count):
    return [pltpu.SemaphoreType.DMA((count,))]


def shards(ways, tables, tokens, norm_gain, in_weight, short_taps, filter_response, skip_gain, out_weight):
    along, across = ways["y"], ways["x"]
    outer = along * across
    cores = ways["co"]
    inner = ways["zl"] * cores
    tp = ways["tp"]
    length, feats = tokens.shape
    chans = skip_gain.shape[0] // inner
    per = chans // outer
    depth, parts = in_weight.shape[0], in_weight.shape[1]
    rows = inner * per
    place = lax.axis_index(INNER)
    where = jnp.stack([lax.axis_index("co"), lax.axis_index("x")]).astype(jnp.int32).reshape(1, 2)

    with jax.named_scope("token_gather"):
        own = lax.all_gather(tokens, ("tp", "zl"), axis=0)
    with jax.named_scope("weight_gather"):
        first = shape((along * inner, parts + 2, depth, LANES), BF16)
        weight = in_weight.transpose(1, 0, 2)
        send = call(
            pack_body,
            first,
            "hhhh",
            (weight, out_weight, filter_response),
            held(weight, out_weight, filter_response, first) + copies_of(4),
        )
        got = lax.all_to_all(send, ("y",) + INNER, 0, 0)
        second = shape((across, along, rows, LANES), BF16)
        here, taps = call(
            repack_body,
            (shape((along * inner, parts + 1, depth, LANES), BF16), second),
            "vhh",
            (got,),
            held(second) + copies_of(2),
        )
        here = here.reshape(along, inner, parts + 1, depth, LANES)
        before = ring(here, "x", across, 1)
        after = ring(here, "x", across, -1)
    with jax.named_scope("token_swap"):
        own, before, after = lax.optimization_barrier((own, before, after))
        other = swap(own, "co")
        tail = own.reshape(tp, ways["zl"], length, feats)[:, -1, length - HALO :]
        halo_own = lax.ppermute(tail, OUTER, [(i, i + 1) for i in range(outer - 1)])
        halo_other = lax.ppermute(
            tail,
            OUTER + ("co",),
            [(i * cores + cores - 1, (i + 1) * cores) for i in range(outer - 1)],
        )
    with jax.named_scope("weight_gather"):
        far_low = ring(before[: along // 2], "x", across, 1)
        far_high = ring(after[along // 2 :], "x", across, -1)
    with jax.named_scope("filter_points"):
        taps = lax.all_to_all(taps, "x", 0, 0)
        points = shape((per * outer * inner, 2 * LANES), F32)
        spec = call(
            filter_body,
            points,
            "vhhhh",
            (taps, tables["into"], tables["near_in"], tables["turn"]),
            held(tables["into"], tables["near_in"], tables["turn"], points) + copies_of(4),
        )
    with jax.named_scope("project"):
        own_taps = lax.dynamic_slice_in_dim(short_taps, place * chans, chans, 2)
        own_taps = own_taps.reshape(short_taps.shape[0], parts * chans)
        stream = shape((inner * length, chans), F32)
        blocks = shape((outer, rows, LANES), BF16)
        out_w = shape((along, across, inner, depth, LANES), BF16)
        held_w = shape((parts,) + out_w.shape, BF16)
        wide = shape((HALO + inner * length, tp * feats), BF16)
        proj = shape((HALO + inner * length, parts * chans), F32)
        query, signal, send, out_w = call(
            functools.partial(project_body, cores),
            (stream, stream, blocks, out_w),
            "shhhhvv" + "h" * 10,
            (where, own, other, halo_own, halo_other, norm_gain.reshape(1, tp * feats), own_taps)
            + (here, before, after, far_low, far_high, spec),
            [pltpu.VMEM((2,) + own.shape, BF16), pltpu.VMEM((2,) + tail.shape, BF16)]
            + held(wide, held_w, proj, stream, stream, blocks)
            + copies_of(4 + 5 * (parts + 1) + 3),
        )
    with jax.named_scope("conv"):
        got = lax.all_to_all(send, OUTER, 0, 0)
        names = ("into", "near_in", "turn", "near_out", "back")
        operands = [spec] + [tables[name] for name in names]
        conv = call(
            conv_body,
            blocks,
            "v" + "h" * (len(operands) + 1),
            (got, *operands),
            held(*operands, blocks) + copies_of(len(operands) + 1),
        )
        conv = lax.all_to_all(conv, OUTER, 0, 0)
    with jax.named_scope("out_weight_gather"):
        out_w = lax.all_gather(out_w.reshape(outer * inner * depth, LANES), INNER, axis=0)
    with jax.named_scope("gate"):
        own_skip = lax.dynamic_slice_in_dim(skip_gain, place * chans, chans, 0)
        gated = call(
            gate_body,
            shape((inner, tp, length, chans), BF16),
            "vhhvv",
            (conv, query, signal, own_skip.reshape(1, chans)),
            held(stream, stream) + copies_of(2),
        )
        gated = lax.all_to_all(
            gated.reshape(inner * tp, length, chans), INNER + ("tp",), 0, 0
        ).reshape(inner, tp, length, chans)
    with jax.named_scope("out_project"):
        return call(
            out_body,
            shape((length, out_weight.shape[1]), BF16),
            "vhv",
            (gated, out_w),
            held(out_w) + copies_of(inner),
        )


def solution(mesh):
    seq, tp = mesh.shape["seq"], mesh.shape["tp"]
    ways = {"y": seq // 16, "x": 4, "zl": 2, "co": 2, "tp": tp}
    fine = Mesh(mesh.devices.reshape(tuple(ways.values())), tuple(ways))
    placed = (
        P(SEQ, "tp"),
        P(),
        P(SEQ, None, "tp"),
        P(None, None, "tp"),
        P(SEQ, "tp"),
        P("tp"),
        P(SEQ, "tp"),
    )

    def run(*args):
        tokens, skip = args[0], args[5]
        inner = ways["zl"] * ways["co"]
        per = skip.shape[0] // (tp * seq)
        tables = transform_tables(tokens.shape[0], per, seq // inner, inner)
        body = functools.partial(shards, ways, tables)
        return jax.shard_map(
            body, mesh=fine, in_specs=placed, out_specs=P(SEQ, "tp"), check_vma=False
        )(*args)

    return run
```

```python
import functools
import math

import jax
import jax.numpy as jnp
import numpy as np
from jax import lax
from jax.experimental import pallas as pl
from jax.experimental.pallas import tpu as pltpu
from jax.sharding import Mesh
from jax.sharding import PartitionSpec as P

F32 = jnp.float32
BF16 = jnp.bfloat16
LANES = 128
HALO = 16
MIB = 1024 * 1024
OUTER = ("y", "x")
INNER = ("zl", "co")
SEQ = OUTER + INNER


def call(body, out_shape, places, args, scratch=(), limit=16):
    spaces = {"h": pltpu.HBM, "v": pltpu.VMEM, "s": pltpu.SMEM}
    specs = [pl.BlockSpec(memory_space=spaces[place]) for place in places]
    single = not isinstance(out_shape, tuple)
    outs = specs[len(args) :]
    return pl.pallas_call(
        body,
        out_shape=out_shape,
        in_specs=specs[: len(args)],
        out_specs=outs[0] if single else tuple(outs),
        scratch_shapes=scratch,
        compiler_params=pltpu.CompilerParams(vmem_limit_bytes=limit * MIB),
    )(*args)


def started(pairs, sems, first=0):
    copies = [
        pltpu.make_async_copy(source, target, sems.at[first + k])
        for k, (source, target) in enumerate(pairs)
    ]
    for copy in copies:
        copy.start()
    return copies


def finish(copies):
    for copy in copies:
        copy.wait()


def transform_tables(length, chans, outer, inner):
    blocks = length // LANES
    row = np.arange(blocks)
    lane = np.arange(LANES)
    far = np.exp(-2j * np.pi * (row[:, None] * (4 * row[None, :] + 1) % (4 * blocks)) / (4 * blocks))
    near = np.exp(-2j * np.pi * (lane[:, None] * lane[None, :] % LANES) / LANES)
    turn = np.exp(-2j * np.pi * ((4 * row[:, None] + 1) * lane[None, :] % (4 * length)) / (4 * length))
    eye = np.eye(chans)
    into = np.einsum("bf,cd->cfbd", far, eye).reshape(chans * blocks, blocks * chans)
    into = np.concatenate([into.real, into.imag], axis=0)
    back = np.einsum("bf,cd->bdcf", far.conj(), eye).reshape(blocks * chans, chans * blocks) / length
    back = np.concatenate([back.real, -back.imag], axis=1)
    near_in = np.block([[near.real, near.imag], [-near.imag, near.real]])
    near_out = np.block([[near.real, -near.imag], [near.imag, near.real]])
    turn = np.stack([turn.real, turn.imag])
    as_short = lambda table: jnp.asarray(table.astype(np.float32)).astype(BF16)
    return {
        "into": as_short(into),
        "back": as_short(back),
        "near_in": as_short(near_in),
        "near_out": as_short(near_out),
        "turn": jnp.asarray(turn.astype(np.float32)),
    }


def times(real, imag, cos, sin):
    return real * cos - imag * sin, real * sin + imag * cos


def turned(pair, turn_ref, sign, axis):
    chans = pair[0].shape[0] // turn_ref.shape[1]
    cos = jnp.concatenate([turn_ref[0]] * chans, axis=0)
    sin = jnp.concatenate([turn_ref[1]] * chans, axis=0) * sign
    return jnp.concatenate(times(*pair, cos, sin), axis=axis).astype(BF16)


def halves(value, axis):
    half = value.shape[axis] // 2
    return lax.slice_in_dim(value, 0, half, axis=axis), lax.slice_in_dim(value, half, 2 * half, axis=axis)


def conv_body(sig_ref, taps_ref, into_ref, near_in_ref, turn_ref, near_out_ref, back_ref, out_ref):
    groups, rows, lanes = sig_ref.shape
    both = jnp.concatenate([sig_ref[...].reshape(groups * rows, lanes), taps_ref[...]], axis=1)
    far = halves(jnp.dot(into_ref[...], both, preferred_element_type=F32), 0)
    sides = [(far[0][:, :lanes], far[1][:, :lanes]), (far[0][:, lanes:], far[1][:, lanes:])]
    pair = jnp.concatenate([turned(side, turn_ref, 1.0, 1) for side in sides], axis=0)
    points = halves(jnp.dot(pair, near_in_ref[...], preferred_element_type=F32), 0)
    product = times(*halves(points[0], 1), *halves(points[1], 1))
    pair = jnp.concatenate(product, axis=1).astype(BF16)
    near = jnp.dot(pair, near_out_ref[...], preferred_element_type=F32)
    pair = turned(halves(near, 1), turn_ref, -1.0, 0)
    result = jnp.dot(back_ref[...], pair, preferred_element_type=F32)
    out_ref[...] = result.astype(BF16).reshape(groups, rows, lanes)


def pack_body(weight_hbm, out_w_hbm, taps_hbm, send_hbm, weight_ref, out_w_ref, taps_ref, send_ref, sems):
    copies = started([(taps_hbm, taps_ref), (weight_hbm, weight_ref), (out_w_hbm, out_w_ref)], sems)
    parts = weight_ref.shape[0]
    total, _, rows, lanes = send_ref.shape
    inner = out_w_ref.shape[1] // lanes
    ways = total // inner
    copies[0].wait()
    for s in range(inner):
        taps = taps_ref[:, s * lanes : (s + 1) * lanes].T.reshape(ways, rows, lanes).astype(BF16)
        for way in range(ways):
            send_ref[way * inner + s, parts + 1] = taps[way]
    finish(copies[1:])
    for s in range(inner):
        at = slice(s * lanes, (s + 1) * lanes)
        for way in range(ways):
            for part in range(parts):
                send_ref[way * inner + s, part] = weight_ref[part, :, at]
            send_ref[way * inner + s, parts] = out_w_ref[:, at]
    finish(started([(send_ref, send_hbm)], sems, len(copies)))


def repack_body(got_ref, send_ref):
    sources, kinds, rows, lanes = got_ref.shape
    ways, tiles = send_ref.shape[0], send_ref.shape[1]
    parts = kinds - 1
    taps = got_ref[:, parts].astype(F32)
    per = rows // ways
    for way in range(ways):
        for part in range(parts):
            send_ref[way, part * sources : (part + 1) * sources] = got_ref[:, part]
        piece = taps[:, way * per : (way + 1) * per].reshape(tiles - parts * sources, rows, lanes)
        send_ref[way, parts * sources :] = piece.astype(BF16)


def project_body(
    cores,
    place_ref,
    own_ref,
    other_ref,
    halo_own_ref,
    halo_other_ref,
    gain_ref,
    taps_ref,
    skip_ref,
    got_ref,
    gates_ref,
    send_ref,
    out_w_ref,
    filter_ref,
    x_ref,
    proj_ref,
):
    core = place_ref[0, 0]
    parts = 3
    ways, _, rows, lanes = got_ref.shape
    groups = send_ref.shape[0]
    outer = groups // ways
    count, chans = gates_ref.shape[0], gates_ref.shape[1] // 2
    inner = count // lanes
    sources = outer * inner

    def column(part):
        pieces = [
            got_ref[x, part * sources + y * inner : part * sources + (y + 1) * inner].reshape(
                inner * rows, lanes
            )
            for y in range(outer)
            for x in range(ways)
        ]
        return jnp.concatenate(pieces, axis=0)

    out_w_ref[...] = column(parts)
    first = (parts + 1) * sources
    for y in range(outer):
        for x in range(ways):
            at = (y * ways + x) * rows
            filter_ref[at : at + rows] = got_ref[x, first + y]

    blocks, length, feats = own_ref.shape
    tp = x_ref.shape[1] // feats

    def put(pieces, at):
        total = sum(jnp.sum(piece * piece, axis=1, keepdims=True) for piece in pieces)
        scale = lax.rsqrt(total / (tp * feats) + 1e-05)
        for p, piece in enumerate(pieces):
            gain = gain_ref[:, p * feats : (p + 1) * feats]
            x_ref[at, p * feats : (p + 1) * feats] = (piece * scale * gain).astype(BF16)

    zs = blocks // tp
    for ref, at_core in ((own_ref, core), (other_ref, cores - 1 - core)):
        for z in range(zs):
            at = pl.multiple_of(HALO + (z * cores + at_core) * length, HALO)
            put([ref[p * zs + z].astype(F32) for p in range(tp)], pl.ds(at, length))
    last = core == cores - 1
    put(
        [jnp.where(last, halo_own_ref[p].astype(F32), halo_other_ref[p].astype(F32)) for p in range(tp)],
        slice(0, HALO),
    )
    weight = jnp.concatenate([column(part) for part in range(parts)], axis=1)
    proj = jnp.dot(x_ref[...], weight, preferred_element_type=F32)
    proj_ref[...] = proj.astype(BF16).astype(F32)

    short = taps_ref[0:1] * proj_ref[HALO:]
    for lag in range(1, taps_ref.shape[0]):
        short = short + taps_ref[lag : lag + 1] * proj_ref[HALO - lag : HALO - lag + count]
    signal = short[:, chans : 2 * chans] * short[:, 2 * chans :]
    gates_ref[:, :chans] = short[:, :chans]
    gates_ref[:, chans:] = skip_ref[...] * signal
    per = send_ref.shape[1] // inner
    pieces = [signal[b * lanes : (b + 1) * lanes].T.reshape(groups, per, lanes) for b in range(inner)]
    send_ref[...] = jnp.concatenate(pieces, axis=1).astype(BF16)


def gate_body(conv_ref, gates_ref, out_ref):
    groups, rows, lanes = conv_ref.shape
    inner = gates_ref.shape[0] // lanes
    per = rows // inner
    chans = groups * per
    conv = conv_ref[...].astype(F32)
    for b in range(inner):
        piece = conv[:, b * per : (b + 1) * per].reshape(chans, lanes).T
        at = slice(b * lanes, (b + 1) * lanes)
        gated = (gates_ref[at, :chans] * (piece + gates_ref[at, chans:])).astype(BF16)
        for p in range(out_ref.shape[1]):
            out_ref[b, p] = gated


def out_body(place_ref, gated_ref, own_ref, near_ref, across_ref, far_ref, out_ref):
    place = place_ref[0, 0]
    inner, tp, rows, chans = gated_ref.shape
    x = jnp.concatenate([gated_ref[s, p] for p in range(tp) for s in range(inner)], axis=1)
    weight = jnp.concatenate([own_ref[...], near_ref[...], across_ref[...], far_ref[...]], axis=1)
    out = jnp.dot(x, weight, preferred_element_type=F32).astype(BF16)
    for k, flip in enumerate((0, 2, 1, 3)):
        at = pl.multiple_of((place ^ flip) * chans, chans)
        out_ref[:, pl.ds(at, chans)] = out[:, k * chans : (k + 1) * chans]


def shape(dims, dtype):
    return jax.ShapeDtypeStruct(dims, dtype)


def swap(value, axis):
    return lax.ppermute(value, axis, [(0, 1), (1, 0)])


def held(*arrays):
    return [pltpu.VMEM(array.shape, array.dtype) for array in arrays]


def copies_of(count):
    return [pltpu.SemaphoreType.DMA((count,))]


def shards(ways, tables, tokens, norm_gain, in_weight, short_taps, filter_response, skip_gain, out_weight):
    along, across = ways["y"], ways["x"]
    outer = along * across
    cores = ways["co"]
    inner = ways["zl"] * cores
    tp = ways["tp"]
    length, feats = tokens.shape
    chans = skip_gain.shape[0] // inner
    per = chans // outer
    depth, parts = in_weight.shape[0], in_weight.shape[1]
    rows = inner * per
    place = lax.axis_index(INNER)
    where = jnp.stack([lax.axis_index("co"), lax.axis_index("x")]).astype(jnp.int32).reshape(1, 2)

    with jax.named_scope("token_gather"):
        own = lax.all_gather(tokens, ("tp", "zl"), axis=0)
    with jax.named_scope("weight_gather"):
        kinds = parts + 2
        first = shape((along * inner, kinds, depth, LANES), BF16)
        weight = in_weight.transpose(1, 0, 2)
        send = call(
            pack_body,
            first,
            "hhhh",
            (weight, out_weight, filter_response),
            held(weight, out_weight, filter_response, first) + copies_of(4),
            limit=60,
        )
        got = lax.all_to_all(send, ("y",) + INNER, 0, 0)
        tiles = (kinds - 1) * along * inner + along
        send = call(repack_body, shape((across, tiles, depth, LANES), BF16), "vv", (got,), limit=56)
        got = lax.all_to_all(send, "x", 0, 0)
    with jax.named_scope("token_swap"):
        own, _ = lax.optimization_barrier((own, send))
        other = swap(own, "co")
        tail = own.reshape(tp, ways["zl"], length, feats)[:, -1, length - HALO :]
        halo_own = lax.ppermute(tail, OUTER, [(i, i + 1) for i in range(outer - 1)])
        halo_other = lax.ppermute(
            tail,
            OUTER + ("co",),
            [(i * cores + cores - 1, (i + 1) * cores) for i in range(outer - 1)],
        )
    with jax.named_scope("project"):
        own_taps = lax.dynamic_slice_in_dim(short_taps, place * chans, chans, 2)
        own_taps = own_taps.reshape(short_taps.shape[0], parts * chans)
        own_skip = lax.dynamic_slice_in_dim(skip_gain, place * chans, chans, 0).reshape(1, chans)
        blocks = shape((outer, rows, LANES), BF16)
        wide = shape((HALO + inner * length, tp * feats), BF16)
        proj = shape((HALO + inner * length, parts * chans), F32)
        gates, send, out_w, taps = call(
            functools.partial(project_body, cores),
            (
                shape((inner * length, 2 * chans), F32),
                blocks,
                shape((outer * inner * depth, chans), BF16),
                shape((outer * rows, LANES), BF16),
            ),
            "s" + "v" * 12,
            (where[:, :1], own, other, halo_own, halo_other)
            + (norm_gain.reshape(1, tp * feats), own_taps, own_skip, got),
            held(wide, proj),
        )
    with jax.named_scope("conv"):
        got = lax.all_to_all(send, OUTER, 0, 0)
        names = ("into", "near_in", "turn", "near_out", "back")
        operands = (got, taps) + tuple(tables[name] for name in names)
        conv = call(conv_body, blocks, "v" * (len(operands) + 1), operands)
        conv = lax.all_to_all(conv, OUTER, 0, 0)
    with jax.named_scope("out_weight_swap"):
        near_w = swap(out_w, "zl")
        across_w = swap(out_w, "co"), swap(near_w, "co")
    with jax.named_scope("gate"):
        gated = call(gate_body, shape((inner, tp, length, chans), BF16), "vvv", (conv, gates))
        gated = lax.all_to_all(
            gated.reshape(inner * tp, length, chans), INNER + ("tp",), 0, 0
        ).reshape(inner, tp, length, chans)
    with jax.named_scope("out_project"):
        return call(
            out_body,
            shape((length, out_weight.shape[1]), BF16),
            "svvvvvv",
            (place.astype(jnp.int32).reshape(1, 1), gated, out_w, near_w, *across_w),
        )


def solution(mesh):
    seq, tp = mesh.shape["seq"], mesh.shape["tp"]
    ways = {"y": seq // 16, "x": 4, "zl": 2, "co": 2, "tp": tp}
    fine = Mesh(mesh.devices.reshape(tuple(ways.values())), tuple(ways))
    placed = (
        P(SEQ, "tp"),
        P(),
        P(SEQ, None, "tp"),
        P(None, None, "tp"),
        P(SEQ, "tp"),
        P("tp"),
        P(SEQ, "tp"),
    )

    def run(*args):
        tokens, skip = args[0], args[5]
        inner = ways["zl"] * ways["co"]
        per = skip.shape[0] // (tp * seq)
        tables = transform_tables(tokens.shape[0], per, seq // inner, inner)
        body = functools.partial(shards, ways, tables)
        return jax.shard_map(
            body, mesh=fine, in_specs=placed, out_specs=P(SEQ, "tp"), check_vma=False
        )(*args)

    return run
```

```python
import functools
import math

import jax
import jax.numpy as jnp
import numpy as np
from jax import lax
from jax.experimental import pallas as pl
from jax.experimental.pallas import tpu as pltpu
from jax.sharding import Mesh
from jax.sharding import PartitionSpec as P

F32 = jnp.float32
BF16 = jnp.bfloat16
LANES = 128
HALO = 16
MIB = 1024 * 1024
OUTER = ("y", "x")
INNER = ("zl", "co")
SEQ = OUTER + INNER


def call(body, out_shape, places, args, scratch=(), limit=16, cost=None):
    spaces = {"h": pltpu.HBM, "v": pltpu.VMEM, "s": pltpu.SMEM}
    specs = [pl.BlockSpec(memory_space=spaces[place]) for place in places]
    single = not isinstance(out_shape, tuple)
    outs = specs[len(args) :]
    return pl.pallas_call(
        body,
        out_shape=out_shape,
        in_specs=specs[: len(args)],
        out_specs=outs[0] if single else tuple(outs),
        scratch_shapes=scratch,
        cost_estimate=cost,
        compiler_params=pltpu.CompilerParams(vmem_limit_bytes=limit * MIB),
    )(*args)


def started(pairs, sems, first=0):
    copies = [
        pltpu.make_async_copy(source, target, sems.at[first + k])
        for k, (source, target) in enumerate(pairs)
    ]
    for copy in copies:
        copy.start()
    return copies


def finish(copies):
    for copy in copies:
        copy.wait()


def transform_tables(length, chans, outer, inner):
    blocks = length // LANES
    row = np.arange(blocks)
    lane = np.arange(LANES)
    far = np.exp(-2j * np.pi * (row[:, None] * (4 * row[None, :] + 1) % (4 * blocks)) / (4 * blocks))
    near = np.exp(-2j * np.pi * (lane[:, None] * lane[None, :] % LANES) / LANES)
    turn = np.exp(-2j * np.pi * ((4 * row[:, None] + 1) * lane[None, :] % (4 * length)) / (4 * length))
    eye = np.eye(chans)
    into = np.einsum("bf,cd->cfbd", far, eye).reshape(chans * blocks, blocks * chans)
    into = np.concatenate([into.real, into.imag], axis=0)
    back = np.einsum("bf,cd->bdcf", far.conj(), eye).reshape(blocks * chans, chans * blocks) / length
    back = np.concatenate([back.real, -back.imag], axis=1)
    near_in = np.block([[near.real, near.imag], [-near.imag, near.real]])
    near_out = np.block([[near.real, -near.imag], [near.imag, near.real]])
    turn = np.stack([turn.real, turn.imag])
    as_short = lambda table: jnp.asarray(table.astype(np.float32)).astype(BF16)
    return {
        "into": as_short(into),
        "back": as_short(back),
        "near_in": as_short(near_in),
        "near_out": as_short(near_out),
        "turn": jnp.asarray(turn.astype(np.float32)),
    }


def times(real, imag, cos, sin):
    return real * cos - imag * sin, real * sin + imag * cos


def turned(pair, turn_ref, sign, axis):
    chans = pair[0].shape[0] // turn_ref.shape[1]
    cos = jnp.concatenate([turn_ref[0]] * chans, axis=0)
    sin = jnp.concatenate([turn_ref[1]] * chans, axis=0) * sign
    return jnp.concatenate(times(*pair, cos, sin), axis=axis).astype(BF16)


def halves(value, axis):
    half = value.shape[axis] // 2
    return lax.slice_in_dim(value, 0, half, axis=axis), lax.slice_in_dim(value, half, 2 * half, axis=axis)


def conv_body(sig_ref, taps_ref, into_ref, near_in_ref, turn_ref, near_out_ref, back_ref, out_ref):
    groups, rows, lanes = sig_ref.shape
    both = jnp.concatenate([sig_ref[...].reshape(groups * rows, lanes), taps_ref[...]], axis=1)
    far = halves(jnp.dot(into_ref[...], both, preferred_element_type=F32), 0)
    sides = [(far[0][:, :lanes], far[1][:, :lanes]), (far[0][:, lanes:], far[1][:, lanes:])]
    pair = jnp.concatenate([turned(side, turn_ref, 1.0, 1) for side in sides], axis=0)
    points = halves(jnp.dot(pair, near_in_ref[...], preferred_element_type=F32), 0)
    product = times(*halves(points[0], 1), *halves(points[1], 1))
    pair = jnp.concatenate(product, axis=1).astype(BF16)
    near = jnp.dot(pair, near_out_ref[...], preferred_element_type=F32)
    pair = turned(halves(near, 1), turn_ref, -1.0, 0)
    result = jnp.dot(back_ref[...], pair, preferred_element_type=F32)
    out_ref[...] = result.astype(BF16).reshape(groups, rows, lanes)


def pack_body(weight_hbm, out_w_hbm, taps_hbm, send_hbm, weight_ref, out_w_ref, taps_ref, send_ref, sems):
    copies = started([(taps_hbm, taps_ref), (weight_hbm, weight_ref), (out_w_hbm, out_w_ref)], sems)
    parts = weight_ref.shape[0]
    total, _, rows, lanes = send_ref.shape
    inner = out_w_ref.shape[1] // lanes
    ways = total // inner
    copies[0].wait()
    for s in range(inner):
        taps = taps_ref[:, s * lanes : (s + 1) * lanes].T.reshape(ways, rows, lanes).astype(BF16)
        for way in range(ways):
            send_ref[way * inner + s, parts + 1] = taps[way]
    finish(copies[1:])
    for s in range(inner):
        at = slice(s * lanes, (s + 1) * lanes)
        for way in range(ways):
            for part in range(parts):
                send_ref[way * inner + s, part] = weight_ref[part, :, at]
            send_ref[way * inner + s, parts] = out_w_ref[:, at]
    finish(started([(send_ref, send_hbm)], sems, len(copies)))


def repack_body(got_ref, send_ref):
    sources, kinds, rows, lanes = got_ref.shape
    ways, tiles = send_ref.shape[0], send_ref.shape[1]
    parts = kinds - 1
    taps = got_ref[:, parts].astype(F32)
    per = rows // ways
    for way in range(ways):
        for part in range(parts):
            send_ref[way, part * sources : (part + 1) * sources] = got_ref[:, part]
        piece = taps[:, way * per : (way + 1) * per].reshape(tiles - parts * sources, rows, lanes)
        send_ref[way, parts * sources :] = piece.astype(BF16)


def project_body(
    cores,
    place_ref,
    own_ref,
    other_ref,
    halo_own_ref,
    halo_other_ref,
    gain_ref,
    taps_ref,
    skip_ref,
    got_ref,
    gates_ref,
    send_ref,
    out_w_ref,
    filter_ref,
    x_ref,
    proj_ref,
):
    core = place_ref[0, 0]
    parts = 3
    ways, _, rows, lanes = got_ref.shape
    groups = send_ref.shape[0]
    outer = groups // ways
    count, chans = gates_ref.shape[0], gates_ref.shape[1] // 2
    inner = count // lanes
    sources = outer * inner

    def column(part):
        pieces = [
            got_ref[x, part * sources + y * inner : part * sources + (y + 1) * inner].reshape(
                inner * rows, lanes
            )
            for y in range(outer)
            for x in range(ways)
        ]
        return jnp.concatenate(pieces, axis=0)

    out_w_ref[...] = column(parts)
    first = (parts + 1) * sources
    for y in range(outer):
        for x in range(ways):
            at = (y * ways + x) * rows
            filter_ref[at : at + rows] = got_ref[x, first + y]

    blocks, length, feats = own_ref.shape
    tp = x_ref.shape[1] // feats

    def put(pieces, at):
        total = sum(jnp.sum(piece * piece, axis=1, keepdims=True) for piece in pieces)
        scale = lax.rsqrt(total / (tp * feats) + 1e-05)
        for p, piece in enumerate(pieces):
            gain = gain_ref[:, p * feats : (p + 1) * feats]
            x_ref[at, p * feats : (p + 1) * feats] = (piece * scale * gain).astype(BF16)

    zs = blocks // tp
    for ref, at_core in ((own_ref, core), (other_ref, cores - 1 - core)):
        for z in range(zs):
            at = pl.multiple_of(HALO + (z * cores + at_core) * length, HALO)
            put([ref[p * zs + z].astype(F32) for p in range(tp)], pl.ds(at, length))
    last = core == cores - 1
    put(
        [jnp.where(last, halo_own_ref[p].astype(F32), halo_other_ref[p].astype(F32)) for p in range(tp)],
        slice(0, HALO),
    )
    weight = jnp.concatenate([column(part) for part in range(parts)], axis=1)
    proj = jnp.dot(x_ref[...], weight, preferred_element_type=F32)
    proj_ref[...] = proj.astype(BF16).astype(F32)

    short = taps_ref[0:1] * proj_ref[HALO:]
    for lag in range(1, taps_ref.shape[0]):
        short = short + taps_ref[lag : lag + 1] * proj_ref[HALO - lag : HALO - lag + count]
    signal = short[:, chans : 2 * chans] * short[:, 2 * chans :]
    gates_ref[:, :chans] = short[:, :chans]
    gates_ref[:, chans:] = skip_ref[...] * signal
    per = send_ref.shape[1] // inner
    pieces = [signal[b * lanes : (b + 1) * lanes].T.reshape(groups, per, lanes) for b in range(inner)]
    send_ref[...] = jnp.concatenate(pieces, axis=1).astype(BF16)


def tail_body(own_hbm, out_ref, sems):
    step = own_hbm.shape[0] // out_ref.shape[0]
    rows = pl.ds(own_hbm.shape[1] - HALO, HALO)
    finish(
        started([(own_hbm.at[step * p + step - 1, rows], out_ref.at[p]) for p in range(out_ref.shape[0])], sems)
    )


def gate_body(conv_ref, gates_ref, out_ref):
    groups, rows, lanes = conv_ref.shape
    inner = gates_ref.shape[0] // lanes
    per = rows // inner
    chans = groups * per
    conv = conv_ref[...].astype(F32)
    for b in range(inner):
        piece = conv[:, b * per : (b + 1) * per].reshape(chans, lanes).T
        at = slice(b * lanes, (b + 1) * lanes)
        gated = (gates_ref[at, :chans] * (piece + gates_ref[at, chans:])).astype(BF16)
        for p in range(out_ref.shape[1]):
            out_ref[b, p] = gated


def out_body(place_ref, gated_ref, own_ref, near_ref, across_ref, far_ref, out_ref):
    place = place_ref[0, 0]
    inner, tp, rows, chans = gated_ref.shape
    x = jnp.concatenate([gated_ref[s, p] for p in range(tp) for s in range(inner)], axis=1)
    weight = jnp.concatenate([own_ref[...], near_ref[...], across_ref[...], far_ref[...]], axis=1)
    out = jnp.dot(x, weight, preferred_element_type=F32).astype(BF16)
    for k, flip in enumerate((0, 2, 1, 3)):
        at = pl.multiple_of((place ^ flip) * chans, chans)
        out_ref[:, pl.ds(at, chans)] = out[:, k * chans : (k + 1) * chans]


def shape(dims, dtype):
    return jax.ShapeDtypeStruct(dims, dtype)


def swap(value, axis):
    return lax.ppermute(value, axis, [(0, 1), (1, 0)])


def held(*arrays):
    return [pltpu.VMEM(array.shape, array.dtype) for array in arrays]


def copies_of(count):
    return [pltpu.SemaphoreType.DMA((count,))]


def shards(ways, tables, tokens, norm_gain, in_weight, short_taps, filter_response, skip_gain, out_weight):
    along, across = ways["y"], ways["x"]
    outer = along * across
    cores = ways["co"]
    inner = ways["zl"] * cores
    tp = ways["tp"]
    length, feats = tokens.shape
    chans = skip_gain.shape[0] // inner
    per = chans // outer
    depth, parts = in_weight.shape[0], in_weight.shape[1]
    rows = inner * per
    place = lax.axis_index(INNER)
    where = jnp.stack([lax.axis_index("co"), lax.axis_index("x")]).astype(jnp.int32).reshape(1, 2)

    with jax.named_scope("token_gather"):
        own = lax.all_gather(tokens, ("tp", "zl"), axis=0)
    with jax.named_scope("weight_gather"):
        kinds = parts + 2
        first = shape((along * inner, kinds, depth, LANES), BF16)
        weight = in_weight.transpose(1, 0, 2)
        send = call(
            pack_body,
            first,
            "hhhh",
            (weight, out_weight, filter_response),
            held(weight, out_weight, filter_response, first) + copies_of(4),
            limit=60,
        )
        got = lax.all_to_all(send, ("y",) + INNER, 0, 0)
        tiles = (kinds - 1) * along * inner + along
        send = call(repack_body, shape((across, tiles, depth, LANES), BF16), "vv", (got,))
        got = lax.all_to_all(send, "x", 0, 0)
    with jax.named_scope("token_swap"):
        own, _ = lax.optimization_barrier((own, send))
        other = swap(own, "co")
        tail = call(
            tail_body,
            shape((tp, HALO, feats), BF16),
            "hv",
            (own,),
            copies_of(tp),
            limit=60,
            cost=pl.CostEstimate(flops=20000000000, bytes_accessed=2 * own.size, transcendentals=0),
        )
        halo_own = lax.ppermute(tail, OUTER, [(i, i + 1) for i in range(outer - 1)])
        halo_other = lax.ppermute(
            tail,
            OUTER + ("co",),
            [(i * cores + cores - 1, (i + 1) * cores) for i in range(outer - 1)],
        )
    with jax.named_scope("project"):
        own_taps = lax.dynamic_slice_in_dim(short_taps, place * chans, chans, 2)
        own_taps = own_taps.reshape(short_taps.shape[0], parts * chans)
        own_skip = lax.dynamic_slice_in_dim(skip_gain, place * chans, chans, 0).reshape(1, chans)
        blocks = shape((outer, rows, LANES), BF16)
        wide = shape((HALO + inner * length, tp * feats), BF16)
        proj = shape((HALO + inner * length, parts * chans), F32)
        gates, send, out_w, taps = call(
            functools.partial(project_body, cores),
            (
                shape((inner * length, 2 * chans), F32),
                blocks,
                shape((outer * inner * depth, chans), BF16),
                shape((outer * rows, LANES), BF16),
            ),
            "s" + "v" * 12,
            (where[:, :1], own, other, halo_own, halo_other)
            + (norm_gain.reshape(1, tp * feats), own_taps, own_skip, got),
            held(wide, proj),
        )
    with jax.named_scope("conv"):
        got = lax.all_to_all(send, OUTER, 0, 0)
        names = ("into", "near_in", "turn", "near_out", "back")
        operands = (got, taps) + tuple(tables[name] for name in names)
        conv = call(conv_body, blocks, "v" * (len(operands) + 1), operands)
        conv = lax.all_to_all(conv, OUTER, 0, 0)
    with jax.named_scope("out_weight_swap"):
        near_w = swap(out_w, "zl")
        across_w = swap(out_w, "co"), swap(near_w, "co")
    with jax.named_scope("gate"):
        gated = call(gate_body, shape((inner, tp, length, chans), BF16), "vvv", (conv, gates))
        gated = lax.all_to_all(
            gated.reshape(inner * tp, length, chans), INNER + ("tp",), 0, 0
        ).reshape(inner, tp, length, chans)
    with jax.named_scope("out_project"):
        return call(
            out_body,
            shape((length, out_weight.shape[1]), BF16),
            "svvvvvv",
            (place.astype(jnp.int32).reshape(1, 1), gated, out_w, near_w, *across_w),
        )


def solution(mesh):
    seq, tp = mesh.shape["seq"], mesh.shape["tp"]
    ways = {"y": seq // 16, "x": 4, "zl": 2, "co": 2, "tp": tp}
    fine = Mesh(mesh.devices.reshape(tuple(ways.values())), tuple(ways))
    placed = (
        P(SEQ, "tp"),
        P(),
        P(SEQ, None, "tp"),
        P(None, None, "tp"),
        P(SEQ, "tp"),
        P("tp"),
        P(SEQ, "tp"),
    )

    def run(*args):
        tokens, skip = args[0], args[5]
        inner = ways["zl"] * ways["co"]
        per = skip.shape[0] // (tp * seq)
        tables = transform_tables(tokens.shape[0], per, seq // inner, inner)
        body = functools.partial(shards, ways, tables)
        return jax.shard_map(
            body, mesh=fine, in_specs=placed, out_specs=P(SEQ, "tp"), check_vma=False
        )(*args)

    return run
```

```python
import functools
import math

import jax
import jax.numpy as jnp
import numpy as np
from jax import lax
from jax.experimental import pallas as pl
from jax.experimental.pallas import tpu as pltpu
from jax.sharding import Mesh
from jax.sharding import PartitionSpec as P

F32 = jnp.float32
BF16 = jnp.bfloat16
LANES = 128
HALO = 16
MIB = 1024 * 1024
OUTER = ("y", "x")
INNER = ("zl", "co")
SEQ = OUTER + INNER


def call(body, out_shape, places, args, scratch=(), limit=16, cost=None):
    spaces = {"h": pltpu.HBM, "v": pltpu.VMEM, "s": pltpu.SMEM}
    specs = [pl.BlockSpec(memory_space=spaces[place]) for place in places]
    single = not isinstance(out_shape, tuple)
    outs = specs[len(args) :]
    return pl.pallas_call(
        body,
        out_shape=out_shape,
        in_specs=specs[: len(args)],
        out_specs=outs[0] if single else tuple(outs),
        scratch_shapes=scratch,
        cost_estimate=cost,
        compiler_params=pltpu.CompilerParams(vmem_limit_bytes=limit * MIB),
    )(*args)


def started(pairs, sems, first=0):
    copies = [
        pltpu.make_async_copy(source, target, sems.at[first + k])
        for k, (source, target) in enumerate(pairs)
    ]
    for copy in copies:
        copy.start()
    return copies


def finish(copies):
    for copy in copies:
        copy.wait()


def transform_tables(length):
    blocks = length // LANES
    row = np.arange(blocks)
    lane = np.arange(LANES)
    far = np.exp(-2j * np.pi * (row[:, None] * (4 * row[None, :] + 1) % (4 * blocks)) / (4 * blocks))
    near = np.exp(-2j * np.pi * (lane[:, None] * lane[None, :] % LANES) / LANES)
    turn = np.exp(-2j * np.pi * ((4 * row[:, None] + 1) * lane[None, :] % (4 * length)) / (4 * length))
    into = np.concatenate([far.T.real, far.T.imag], axis=0)
    back = np.concatenate([far.real, far.imag], axis=1) / length
    near_in = np.block([[near.real, near.imag], [-near.imag, near.real]])
    near_out = np.block([[near.real, -near.imag], [near.imag, near.real]])
    turn = np.stack([turn.real, turn.imag])
    as_short = lambda table: jnp.asarray(table.astype(np.float32)).astype(BF16)
    return {
        "into": as_short(into),
        "back": as_short(back),
        "near_in": as_short(near_in),
        "near_out": as_short(near_out),
        "turn": jnp.asarray(turn.astype(np.float32)),
    }


def times(real, imag, cos, sin):
    return real * cos - imag * sin, real * sin + imag * cos


def halves(value, axis):
    half = value.shape[axis] // 2
    return lax.slice_in_dim(value, 0, half, axis=axis), lax.slice_in_dim(value, half, 2 * half, axis=axis)


def conv_body(
    sig_ref,
    taps_ref,
    into_ref,
    near_in_ref,
    turn_ref,
    near_out_ref,
    back_ref,
    earlier_ref,
    out_ref,
    both_ref,
    result_ref,
):
    groups, rows, lanes = sig_ref.shape
    blocks = into_ref.shape[1]
    per = groups * rows // blocks
    both_ref[0] = sig_ref[...].reshape(groups * rows, lanes).astype(F32)
    both_ref[1] = taps_ref[...].astype(F32)
    cos, sin = turn_ref[0], turn_ref[1]
    pairs = []
    for chan in range(per):
        at = pl.ds(chan, blocks, stride=per)
        both = jnp.concatenate([both_ref[0, at], both_ref[1, at]], axis=1).astype(BF16)
        far = jnp.dot(into_ref[...], both, preferred_element_type=F32)
        real, imag = halves(far, 0)
        pairs += [
            jnp.concatenate(times(r, i, cos, sin), axis=1)
            for r, i in zip(halves(real, 1), halves(imag, 1))
        ]
    pair = jnp.concatenate(pairs[::2] + pairs[1::2], axis=0).astype(BF16)
    points = halves(jnp.dot(pair, near_in_ref[...], preferred_element_type=F32), 0)
    product = times(*halves(points[0], 1), *halves(points[1], 1))
    pair = jnp.concatenate(product, axis=1).astype(BF16)
    near = jnp.dot(pair, near_out_ref[...], preferred_element_type=F32)
    for chan in range(per):
        real, imag = halves(near[chan * blocks : (chan + 1) * blocks], 1)
        pair = jnp.concatenate(times(real, imag, cos, -sin), axis=0).astype(BF16)
        at = pl.ds(chan, blocks, stride=per)
        result_ref[at] = jnp.dot(back_ref[...], pair, preferred_element_type=F32)
    out_ref[...] = result_ref[...].astype(BF16).reshape(groups, rows, lanes)


def pack_body(weight_hbm, out_w_hbm, taps_hbm, send_hbm, weight_ref, out_w_ref, taps_ref, send_ref, sems):
    copies = started([(taps_hbm, taps_ref), (weight_hbm, weight_ref), (out_w_hbm, out_w_ref)], sems)
    parts = weight_ref.shape[0]
    total, _, rows, lanes = send_ref.shape
    inner = out_w_ref.shape[1] // lanes
    ways = total // inner
    copies[0].wait()
    for s in range(inner):
        taps = taps_ref[:, s * lanes : (s + 1) * lanes].T.reshape(ways, rows, lanes).astype(BF16)
        for way in range(ways):
            send_ref[way * inner + s, parts + 1] = taps[way]
    finish(copies[1:])
    for s in range(inner):
        at = slice(s * lanes, (s + 1) * lanes)
        for way in range(ways):
            for part in range(parts):
                send_ref[way * inner + s, part] = weight_ref[part, :, at]
            send_ref[way * inner + s, parts] = out_w_ref[:, at]
    finish(started([(send_ref, send_hbm)], sems, len(copies)))


def repack_body(got_ref, send_ref):
    sources, kinds, rows, lanes = got_ref.shape
    ways, tiles = send_ref.shape[0], send_ref.shape[1]
    parts = kinds - 1
    taps = got_ref[:, parts].astype(F32)
    per = rows // ways
    for way in range(ways):
        for part in range(parts):
            send_ref[way, part * sources : (part + 1) * sources] = got_ref[:, part]
        piece = taps[:, way * per : (way + 1) * per].reshape(tiles - parts * sources, rows, lanes)
        send_ref[way, parts * sources :] = piece.astype(BF16)


def project_body(
    cores,
    place_ref,
    own_ref,
    other_ref,
    halo_own_ref,
    halo_other_ref,
    gain_ref,
    taps_ref,
    skip_ref,
    got_ref,
    gates_ref,
    send_ref,
    out_w_ref,
    filter_ref,
    x_ref,
    proj_ref,
):
    core = place_ref[0, 0]
    parts = 3
    ways, _, rows, lanes = got_ref.shape
    groups = send_ref.shape[0]
    outer = groups // ways
    count, chans = gates_ref.shape[0], gates_ref.shape[1] // 2
    inner = count // lanes
    sources = outer * inner

    def column(part):
        pieces = [
            got_ref[x, part * sources + y * inner : part * sources + (y + 1) * inner].reshape(
                inner * rows, lanes
            )
            for y in range(outer)
            for x in range(ways)
        ]
        return jnp.concatenate(pieces, axis=0)

    out_w_ref[...] = column(parts)
    first = (parts + 1) * sources
    for y in range(outer):
        for x in range(ways):
            at = (y * ways + x) * rows
            filter_ref[at : at + rows] = got_ref[x, first + y]

    blocks, length, feats = own_ref.shape
    tp = x_ref.shape[1] // feats

    def put(pieces, at):
        total = sum(jnp.sum(piece * piece, axis=1, keepdims=True) for piece in pieces)
        scale = lax.rsqrt(total / (tp * feats) + 1e-05)
        for p, piece in enumerate(pieces):
            gain = gain_ref[:, p * feats : (p + 1) * feats]
            x_ref[at, p * feats : (p + 1) * feats] = (piece * scale * gain).astype(BF16)

    zs = blocks // tp
    for ref, at_core in ((own_ref, core), (other_ref, cores - 1 - core)):
        for z in range(zs):
            at = pl.multiple_of(HALO + (z * cores + at_core) * length, HALO)
            put([ref[p * zs + z].astype(F32) for p in range(tp)], pl.ds(at, length))
    last = core == cores - 1
    put(
        [jnp.where(last, halo_own_ref[p].astype(F32), halo_other_ref[p].astype(F32)) for p in range(tp)],
        slice(0, HALO),
    )
    weight = jnp.concatenate([column(part) for part in range(parts)], axis=1)
    proj = jnp.dot(x_ref[...], weight, preferred_element_type=F32)
    proj_ref[...] = proj.astype(BF16).astype(F32)

    short = taps_ref[0:1] * proj_ref[HALO:]
    for lag in range(1, taps_ref.shape[0]):
        short = short + taps_ref[lag : lag + 1] * proj_ref[HALO - lag : HALO - lag + count]
    signal = short[:, chans : 2 * chans] * short[:, 2 * chans :]
    gates_ref[:, :chans] = short[:, :chans]
    gates_ref[:, chans:] = skip_ref[...] * signal
    per = send_ref.shape[1] // inner
    pieces = [signal[b * lanes : (b + 1) * lanes].T.reshape(groups, per, lanes) for b in range(inner)]
    send_ref[...] = jnp.concatenate(pieces, axis=1).astype(BF16)


def tail_body(own_hbm, out_ref, sems):
    step = own_hbm.shape[0] // out_ref.shape[0]
    rows = pl.ds(own_hbm.shape[1] - HALO, HALO)
    finish(
        started([(own_hbm.at[step * p + step - 1, rows], out_ref.at[p]) for p in range(out_ref.shape[0])], sems)
    )


def gate_body(conv_ref, gates_ref, out_ref):
    groups, rows, lanes = conv_ref.shape
    inner = gates_ref.shape[0] // lanes
    per = rows // inner
    chans = groups * per
    conv = conv_ref[...].astype(F32)
    for b in range(inner):
        piece = conv[:, b * per : (b + 1) * per].reshape(chans, lanes).T
        at = slice(b * lanes, (b + 1) * lanes)
        gated = (gates_ref[at, :chans] * (piece + gates_ref[at, chans:])).astype(BF16)
        for p in range(out_ref.shape[1]):
            out_ref[b, p] = gated


def out_body(place_ref, gated_ref, own_ref, near_ref, across_ref, far_ref, out_ref):
    place = place_ref[0, 0]
    inner, tp, rows, chans = gated_ref.shape
    x = jnp.concatenate([gated_ref[s, p] for p in range(tp) for s in range(inner)], axis=1)
    weight = jnp.concatenate([own_ref[...], near_ref[...], across_ref[...], far_ref[...]], axis=1)
    out = jnp.dot(x, weight, preferred_element_type=F32).astype(BF16)
    for k, flip in enumerate((0, 2, 1, 3)):
        at = pl.multiple_of((place ^ flip) * chans, chans)
        out_ref[:, pl.ds(at, chans)] = out[:, k * chans : (k + 1) * chans]


def shape(dims, dtype):
    return jax.ShapeDtypeStruct(dims, dtype)


def swap(value, axis):
    return lax.ppermute(value, axis, [(0, 1), (1, 0)])


def held(*arrays):
    return [pltpu.VMEM(array.shape, array.dtype) for array in arrays]


def copies_of(count):
    return [pltpu.SemaphoreType.DMA((count,))]


def shards(ways, tables, tokens, norm_gain, in_weight, short_taps, filter_response, skip_gain, out_weight):
    along, across = ways["y"], ways["x"]
    outer = along * across
    cores = ways["co"]
    inner = ways["zl"] * cores
    tp = ways["tp"]
    length, feats = tokens.shape
    chans = skip_gain.shape[0] // inner
    per = chans // outer
    depth, parts = in_weight.shape[0], in_weight.shape[1]
    rows = inner * per
    place = lax.axis_index(INNER)
    where = jnp.stack([lax.axis_index("co"), lax.axis_index("x")]).astype(jnp.int32).reshape(1, 2)

    with jax.named_scope("token_gather"):
        own = lax.all_gather(tokens, ("tp", "zl"), axis=0)
    with jax.named_scope("weight_gather"):
        kinds = parts + 2
        first = shape((along * inner, kinds, depth, LANES), BF16)
        weight = in_weight.transpose(1, 0, 2)
        send = call(
            pack_body,
            first,
            "hhhh",
            (weight, out_weight, filter_response),
            held(weight, out_weight, filter_response, first) + copies_of(4),
            limit=60,
        )
        got = lax.all_to_all(send, ("y",) + INNER, 0, 0)
        tiles = (kinds - 1) * along * inner + along
        send = call(repack_body, shape((across, tiles, depth, LANES), BF16), "vv", (got,))
        got = lax.all_to_all(send, "x", 0, 0)
    with jax.named_scope("token_swap"):
        own, _ = lax.optimization_barrier((own, send))
        other = swap(own, "co")
        tail = call(
            tail_body,
            shape((tp, HALO, feats), BF16),
            "hv",
            (own,),
            copies_of(tp),
            limit=60,
            cost=pl.CostEstimate(flops=20000000000, bytes_accessed=2 * own.size, transcendentals=0),
        )
        halo_own = lax.ppermute(tail, OUTER, [(i, i + 1) for i in range(outer - 1)])
        halo_other = lax.ppermute(
            tail,
            OUTER + ("co",),
            [(i * cores + cores - 1, (i + 1) * cores) for i in range(outer - 1)],
        )
    with jax.named_scope("project"):
        own_taps = lax.dynamic_slice_in_dim(short_taps, place * chans, chans, 2)
        own_taps = own_taps.reshape(short_taps.shape[0], parts * chans)
        own_skip = lax.dynamic_slice_in_dim(skip_gain, place * chans, chans, 0).reshape(1, chans)
        blocks = shape((outer, rows, LANES), BF16)
        wide = shape((HALO + inner * length, tp * feats), BF16)
        proj = shape((HALO + inner * length, parts * chans), F32)
        gates, send, out_w, taps = call(
            functools.partial(project_body, cores),
            (
                shape((inner * length, 2 * chans), F32),
                blocks,
                shape((outer * inner * depth, chans), BF16),
                shape((outer * rows, LANES), BF16),
            ),
            "s" + "v" * 12,
            (where[:, :1], own, other, halo_own, halo_other)
            + (norm_gain.reshape(1, tp * feats), own_taps, own_skip, got),
            held(wide, proj),
        )
    with jax.named_scope("out_weight_swap"):
        near_w = swap(out_w, "zl")
    with jax.named_scope("conv"):
        got = lax.all_to_all(send, OUTER, 0, 0)
        names = ("into", "near_in", "turn", "near_out", "back")
        operands = (got, taps) + tuple(tables[name] for name in names) + (near_w,)
        count = outer * rows
        held_rows = [pltpu.VMEM((2, count, LANES), F32), pltpu.VMEM((count, LANES), F32)]
        conv = call(conv_body, blocks, "v" * (len(operands) - 1) + "hv", operands, held_rows)
        conv = lax.all_to_all(conv, OUTER, 0, 0)
    with jax.named_scope("out_weight_swap"):
        across_w = swap(out_w, "co"), swap(near_w, "co")
    with jax.named_scope("gate"):
        gated = call(gate_body, shape((inner, tp, length, chans), BF16), "vvv", (conv, gates))
        gated = lax.all_to_all(
            gated.reshape(inner * tp, length, chans), INNER + ("tp",), 0, 0
        ).reshape(inner, tp, length, chans)
    with jax.named_scope("out_project"):
        return call(
            out_body,
            shape((length, out_weight.shape[1]), BF16),
            "svvvvvv",
            (place.astype(jnp.int32).reshape(1, 1), gated, out_w, near_w, *across_w),
        )


def solution(mesh):
    seq, tp = mesh.shape["seq"], mesh.shape["tp"]
    ways = {"y": seq // 16, "x": 4, "zl": 2, "co": 2, "tp": tp}
    fine = Mesh(mesh.devices.reshape(tuple(ways.values())), tuple(ways))
    placed = (
        P(SEQ, "tp"),
        P(),
        P(SEQ, None, "tp"),
        P(None, None, "tp"),
        P(SEQ, "tp"),
        P("tp"),
        P(SEQ, "tp"),
    )

    def run(*args):
        tables = transform_tables(args[0].shape[0])
        body = functools.partial(shards, ways, tables)
        return jax.shard_map(
            body, mesh=fine, in_specs=placed, out_specs=P(SEQ, "tp"), check_vma=False
        )(*args)

    return run
```

```python
import functools
import math

import jax
import jax.numpy as jnp
import numpy as np
from jax import lax
from jax.experimental import pallas as pl
from jax.experimental.pallas import tpu as pltpu
from jax.sharding import Mesh
from jax.sharding import PartitionSpec as P

F32 = jnp.float32
BF16 = jnp.bfloat16
LANES = 128
HALO = 16
MIB = 1024 * 1024
OUTER = ("y", "x")
INNER = ("zl", "co")
SEQ = OUTER + INNER


def call(body, out_shape, places, args, scratch=(), limit=16, cost=None):
    spaces = {"h": pltpu.HBM, "v": pltpu.VMEM, "s": pltpu.SMEM}
    specs = [pl.BlockSpec(memory_space=spaces[place]) for place in places]
    single = not isinstance(out_shape, tuple)
    outs = specs[len(args) :]
    return pl.pallas_call(
        body,
        out_shape=out_shape,
        in_specs=specs[: len(args)],
        out_specs=outs[0] if single else tuple(outs),
        scratch_shapes=scratch,
        cost_estimate=cost,
        compiler_params=pltpu.CompilerParams(vmem_limit_bytes=limit * MIB),
    )(*args)


def started(pairs, sems, first=0):
    copies = [
        pltpu.make_async_copy(source, target, sems.at[first + k])
        for k, (source, target) in enumerate(pairs)
    ]
    for copy in copies:
        copy.start()
    return copies


def finish(copies):
    for copy in copies:
        copy.wait()


def transform_tables(length):
    blocks = length // LANES
    row = np.arange(blocks)
    lane = np.arange(LANES)
    far = np.exp(-2j * np.pi * (row[:, None] * (4 * row[None, :] + 1) % (4 * blocks)) / (4 * blocks))
    near = np.exp(-2j * np.pi * (lane[:, None] * lane[None, :] % LANES) / LANES)
    turn = np.exp(-2j * np.pi * ((4 * row[:, None] + 1) * lane[None, :] % (4 * length)) / (4 * length))
    into = np.concatenate([far.T.real, far.T.imag], axis=0)
    back = np.concatenate([far.real, far.imag], axis=1) / length
    near_in = np.block([[near.real, near.imag], [-near.imag, near.real]])
    near_out = np.block([[near.real, -near.imag], [near.imag, near.real]])
    turn = np.stack([turn.real, turn.imag])
    as_short = lambda table: jnp.asarray(table.astype(np.float32)).astype(BF16)
    return {
        "into": as_short(into),
        "back": as_short(back),
        "near_in": as_short(near_in),
        "near_out": as_short(near_out),
        "turn": jnp.asarray(turn.astype(np.float32)),
    }


def times(real, imag, cos, sin):
    return real * cos - imag * sin, real * sin + imag * cos


def halves(value, axis):
    half = value.shape[axis] // 2
    return lax.slice_in_dim(value, 0, half, axis=axis), lax.slice_in_dim(value, half, 2 * half, axis=axis)


def conv_body(
    sig_ref,
    taps_ref,
    into_ref,
    near_in_ref,
    turn_ref,
    near_out_ref,
    back_ref,
    out_ref,
    both_ref,
    result_ref,
):
    groups, rows, lanes = sig_ref.shape
    blocks = into_ref.shape[1]
    per = groups * rows // blocks
    both_ref[0] = sig_ref[...].reshape(groups * rows, lanes).astype(F32)
    both_ref[1] = taps_ref[...].astype(F32)
    cos, sin = turn_ref[0], turn_ref[1]
    pairs = []
    for chan in range(per):
        at = pl.ds(chan, blocks, stride=per)
        both = jnp.concatenate([both_ref[0, at], both_ref[1, at]], axis=1).astype(BF16)
        far = jnp.dot(into_ref[...], both, preferred_element_type=F32)
        real, imag = halves(far, 0)
        pairs += [
            jnp.concatenate(times(r, i, cos, sin), axis=1)
            for r, i in zip(halves(real, 1), halves(imag, 1))
        ]
    pair = jnp.concatenate(pairs[::2] + pairs[1::2], axis=0).astype(BF16)
    points = halves(jnp.dot(pair, near_in_ref[...], preferred_element_type=F32), 0)
    product = times(*halves(points[0], 1), *halves(points[1], 1))
    pair = jnp.concatenate(product, axis=1).astype(BF16)
    near = jnp.dot(pair, near_out_ref[...], preferred_element_type=F32)
    for chan in range(per):
        real, imag = halves(near[chan * blocks : (chan + 1) * blocks], 1)
        pair = jnp.concatenate(times(real, imag, cos, -sin), axis=0).astype(BF16)
        at = pl.ds(chan, blocks, stride=per)
        result_ref[at] = jnp.dot(back_ref[...], pair, preferred_element_type=F32)
    out_ref[...] = result_ref[...].astype(BF16).reshape(groups, rows, lanes)


def pack_body(weight_hbm, out_w_hbm, taps_hbm, send_hbm, weight_ref, out_w_ref, taps_ref, send_ref, sems):
    copies = started([(taps_hbm, taps_ref), (weight_hbm, weight_ref), (out_w_hbm, out_w_ref)], sems)
    parts = weight_ref.shape[0]
    total, _, rows, lanes = send_ref.shape
    inner = out_w_ref.shape[1] // lanes
    ways = total // inner
    copies[0].wait()
    for s in range(inner):
        taps = taps_ref[:, s * lanes : (s + 1) * lanes].T.reshape(ways, rows, lanes).astype(BF16)
        for way in range(ways):
            send_ref[way * inner + s, parts + 1] = taps[way]
    finish(copies[1:])
    for s in range(inner):
        at = slice(s * lanes, (s + 1) * lanes)
        for way in range(ways):
            for part in range(parts):
                send_ref[way * inner + s, part] = weight_ref[part, :, at]
            send_ref[way * inner + s, parts] = out_w_ref[:, at]
    finish(started([(send_ref, send_hbm)], sems, len(copies)))


def repack_body(got_ref, send_ref, out_w_ref):
    sources, kinds, rows, lanes = got_ref.shape
    ways, tiles = send_ref.shape[0], send_ref.shape[1]
    parts = kinds - 2
    out_w_ref[...] = got_ref[:, parts]
    taps = got_ref[:, parts + 1].astype(F32)
    per = rows // ways
    for way in range(ways):
        for part in range(parts):
            send_ref[way, part * sources : (part + 1) * sources] = got_ref[:, part]
        piece = taps[:, way * per : (way + 1) * per].reshape(tiles - parts * sources, rows, lanes)
        send_ref[way, parts * sources :] = piece.astype(BF16)


def project_body(
    cores,
    place_ref,
    own_ref,
    other_ref,
    halo_own_ref,
    halo_other_ref,
    gain_ref,
    taps_ref,
    skip_ref,
    got_ref,
    gates_ref,
    send_ref,
    filter_ref,
    x_ref,
    proj_ref,
):
    core = place_ref[0, 0]
    parts = 3
    ways, _, rows, lanes = got_ref.shape
    groups = send_ref.shape[0]
    outer = groups // ways
    count, chans = gates_ref.shape[0], gates_ref.shape[1] // 2
    inner = count // lanes
    sources = outer * inner

    def column(part):
        pieces = [
            got_ref[x, part * sources + y * inner : part * sources + (y + 1) * inner].reshape(
                inner * rows, lanes
            )
            for y in range(outer)
            for x in range(ways)
        ]
        return jnp.concatenate(pieces, axis=0)

    first = parts * sources
    for y in range(outer):
        for x in range(ways):
            at = (y * ways + x) * rows
            filter_ref[at : at + rows] = got_ref[x, first + y]

    blocks, length, feats = own_ref.shape
    tp = x_ref.shape[1] // feats

    def put(pieces, at):
        total = sum(jnp.sum(piece * piece, axis=1, keepdims=True) for piece in pieces)
        scale = lax.rsqrt(total / (tp * feats) + 1e-05)
        for p, piece in enumerate(pieces):
            gain = gain_ref[:, p * feats : (p + 1) * feats]
            x_ref[at, p * feats : (p + 1) * feats] = (piece * scale * gain).astype(BF16)

    zs = blocks // tp
    for ref, at_core in ((own_ref, core), (other_ref, cores - 1 - core)):
        for z in range(zs):
            at = pl.multiple_of(HALO + (z * cores + at_core) * length, HALO)
            put([ref[p * zs + z].astype(F32) for p in range(tp)], pl.ds(at, length))
    last = core == cores - 1
    put(
        [jnp.where(last, halo_own_ref[p].astype(F32), halo_other_ref[p].astype(F32)) for p in range(tp)],
        slice(0, HALO),
    )
    weight = jnp.concatenate([column(part) for part in range(parts)], axis=1)
    proj = jnp.dot(x_ref[...], weight, preferred_element_type=F32)
    proj_ref[...] = proj.astype(BF16).astype(F32)

    short = taps_ref[0:1] * proj_ref[HALO:]
    for lag in range(1, taps_ref.shape[0]):
        short = short + taps_ref[lag : lag + 1] * proj_ref[HALO - lag : HALO - lag + count]
    signal = short[:, chans : 2 * chans] * short[:, 2 * chans :]
    gates_ref[:, :chans] = short[:, :chans]
    gates_ref[:, chans:] = skip_ref[...] * signal
    per = send_ref.shape[1] // inner
    pieces = [signal[b * lanes : (b + 1) * lanes].T.reshape(groups, per, lanes) for b in range(inner)]
    send_ref[...] = jnp.concatenate(pieces, axis=1).astype(BF16)


def tail_body(own_hbm, out_ref, sems):
    step = own_hbm.shape[0] // out_ref.shape[0]
    rows = pl.ds(own_hbm.shape[1] - HALO, HALO)
    finish(
        started([(own_hbm.at[step * p + step - 1, rows], out_ref.at[p]) for p in range(out_ref.shape[0])], sems)
    )


def gate_body(conv_ref, gates_ref, out_ref):
    groups, rows, lanes = conv_ref.shape
    inner = gates_ref.shape[0] // lanes
    per = rows // inner
    chans = groups * per
    conv = conv_ref[...].astype(F32)
    for b in range(inner):
        piece = conv[:, b * per : (b + 1) * per].reshape(chans, lanes).T
        at = slice(b * lanes, (b + 1) * lanes)
        gated = (gates_ref[at, :chans] * (piece + gates_ref[at, chans:])).astype(BF16)
        for p in range(out_ref.shape[1]):
            out_ref[b, p] = gated


def out_body(core_ref, gated_ref, own_ref, other_ref, out_ref):
    core = core_ref[0, 0]
    inner, tp, rows, chans = gated_ref.shape
    cores = other_ref.shape[0] // own_ref.shape[0] + 1
    zs = inner // cores
    ways = own_ref.shape[0] // zs
    x = jnp.concatenate([gated_ref[s, p] for p in range(tp) for s in range(inner)], axis=1)

    def column(ref, z):
        pieces = [ref[x * zs + z, y] for y in range(ref.shape[1]) for x in range(ways)]
        return jnp.concatenate(pieces, axis=0)

    weight = jnp.concatenate([column(ref, z) for ref in (own_ref, other_ref) for z in range(zs)], axis=1)
    out = jnp.dot(x, weight, preferred_element_type=F32).astype(BF16)
    for side, at_core in enumerate((core, cores - 1 - core)):
        for z in range(zs):
            k = side * zs + z
            at = pl.multiple_of((z * cores + at_core) * chans, chans)
            out_ref[:, pl.ds(at, chans)] = out[:, k * chans : (k + 1) * chans]


def shape(dims, dtype):
    return jax.ShapeDtypeStruct(dims, dtype)


def swap(value, axis):
    return lax.ppermute(value, axis, [(0, 1), (1, 0)])


def held(*arrays):
    return [pltpu.VMEM(array.shape, array.dtype) for array in arrays]


def copies_of(count):
    return [pltpu.SemaphoreType.DMA((count,))]


def shards(ways, tables, tokens, norm_gain, in_weight, short_taps, filter_response, skip_gain, out_weight):
    along, across = ways["y"], ways["x"]
    outer = along * across
    cores = ways["co"]
    inner = ways["zl"] * cores
    tp = ways["tp"]
    length, feats = tokens.shape
    chans = skip_gain.shape[0] // inner
    per = chans // outer
    depth, parts = in_weight.shape[0], in_weight.shape[1]
    rows = inner * per
    place = lax.axis_index(INNER)
    where = jnp.stack([lax.axis_index("co"), lax.axis_index("x")]).astype(jnp.int32).reshape(1, 2)

    with jax.named_scope("token_gather"):
        own = lax.all_gather(tokens, ("tp", "zl"), axis=0)
    with jax.named_scope("weight_gather"):
        kinds = parts + 2
        first = shape((along * inner, kinds, depth, LANES), BF16)
        weight = in_weight.transpose(1, 0, 2)
        send = call(
            pack_body,
            first,
            "hhhh",
            (weight, out_weight, filter_response),
            held(weight, out_weight, filter_response, first) + copies_of(4),
            limit=60,
        )
        got = lax.all_to_all(send, ("y",) + INNER, 0, 0)
        tiles = parts * along * inner + along
        piece_w = shape((along * inner, depth, LANES), BF16)
        send, piece = call(
            repack_body, (shape((across, tiles, depth, LANES), BF16), piece_w), "vvv", (got,)
        )
        got = lax.all_to_all(send, "x", 0, 0)
    with jax.named_scope("token_swap"):
        own, _ = lax.optimization_barrier((own, send))
        other = swap(own, "co")
        tail = call(
            tail_body,
            shape((tp, HALO, feats), BF16),
            "hv",
            (own,),
            copies_of(tp),
            limit=60,
            cost=pl.CostEstimate(flops=20000000000, bytes_accessed=2 * own.size, transcendentals=0),
        )
        halo_own = lax.ppermute(tail, OUTER, [(i, i + 1) for i in range(outer - 1)])
        halo_other = lax.ppermute(
            tail,
            OUTER + ("co",),
            [(i * cores + cores - 1, (i + 1) * cores) for i in range(outer - 1)],
        )
    with jax.named_scope("out_weight_gather"):
        out_w = lax.all_gather(piece.reshape(along, inner * depth, LANES), ("x", "zl"), axis=0)
    with jax.named_scope("project"):
        own_taps = lax.dynamic_slice_in_dim(short_taps, place * chans, chans, 2)
        own_taps = own_taps.reshape(short_taps.shape[0], parts * chans)
        own_skip = lax.dynamic_slice_in_dim(skip_gain, place * chans, chans, 0).reshape(1, chans)
        blocks = shape((outer, rows, LANES), BF16)
        wide = shape((HALO + inner * length, tp * feats), BF16)
        proj = shape((HALO + inner * length, parts * chans), F32)
        gates, send, taps = call(
            functools.partial(project_body, cores),
            (
                shape((inner * length, 2 * chans), F32),
                blocks,
                shape((outer * rows, LANES), BF16),
            ),
            "s" + "v" * 11,
            (where[:, :1], own, other, halo_own, halo_other)
            + (norm_gain.reshape(1, tp * feats), own_taps, own_skip, got),
            held(wide, proj),
        )
    with jax.named_scope("conv"):
        got = lax.all_to_all(send, OUTER, 0, 0)
        names = ("into", "near_in", "turn", "near_out", "back")
        operands = (got, taps) + tuple(tables[name] for name in names)
        count = outer * rows
        held_rows = [pltpu.VMEM((2, count, LANES), F32), pltpu.VMEM((count, LANES), F32)]
        conv = call(conv_body, blocks, "v" * (len(operands) + 1), operands, held_rows)
        conv = lax.all_to_all(conv, OUTER, 0, 0)
    with jax.named_scope("out_weight_swap"):
        other_w = swap(out_w, "co")
    with jax.named_scope("gate"):
        gated = call(gate_body, shape((inner, tp, length, chans), BF16), "vvv", (conv, gates))
        gated = lax.all_to_all(
            gated.reshape(inner * tp, length, chans), INNER + ("tp",), 0, 0
        ).reshape(inner, tp, length, chans)
    with jax.named_scope("out_project"):
        return call(
            out_body,
            shape((length, out_weight.shape[1]), BF16),
            "svvvv",
            (where[:, :1], gated, out_w, other_w),
        )


def solution(mesh):
    seq, tp = mesh.shape["seq"], mesh.shape["tp"]
    ways = {"y": seq // 16, "x": 4, "zl": 2, "co": 2, "tp": tp}
    fine = Mesh(mesh.devices.reshape(tuple(ways.values())), tuple(ways))
    placed = (
        P(SEQ, "tp"),
        P(),
        P(SEQ, None, "tp"),
        P(None, None, "tp"),
        P(SEQ, "tp"),
        P("tp"),
        P(SEQ, "tp"),
    )

    def run(*args):
        tables = transform_tables(args[0].shape[0])
        body = functools.partial(shards, ways, tables)
        return jax.shard_map(
            body, mesh=fine, in_specs=placed, out_specs=P(SEQ, "tp"), check_vma=False
        )(*args)

    return run
```

```python
import functools
import math

import jax
import jax.numpy as jnp
import numpy as np
from jax import lax
from jax.experimental import pallas as pl
from jax.experimental.pallas import tpu as pltpu
from jax.sharding import Mesh
from jax.sharding import PartitionSpec as P

F32 = jnp.float32
BF16 = jnp.bfloat16
LANES = 128
HALO = 16
MIB = 1024 * 1024
OUTER = ("y", "x")
INNER = ("zl", "co")
SEQ = OUTER + INNER


def call(body, out_shape, places, args, scratch=(), limit=16, cost=None):
    spaces = {"h": pltpu.HBM, "v": pltpu.VMEM, "s": pltpu.SMEM}
    specs = [pl.BlockSpec(memory_space=spaces[place]) for place in places]
    single = not isinstance(out_shape, tuple)
    outs = specs[len(args) :]
    return pl.pallas_call(
        body,
        out_shape=out_shape,
        in_specs=specs[: len(args)],
        out_specs=outs[0] if single else tuple(outs),
        scratch_shapes=scratch,
        cost_estimate=cost,
        compiler_params=pltpu.CompilerParams(vmem_limit_bytes=limit * MIB),
    )(*args)


def started(pairs, sems, first=0):
    copies = [
        pltpu.make_async_copy(source, target, sems.at[first + k])
        for k, (source, target) in enumerate(pairs)
    ]
    for copy in copies:
        copy.start()
    return copies


def finish(copies):
    for copy in copies:
        copy.wait()


def transform_tables(length):
    blocks = length // LANES
    row = np.arange(blocks)
    lane = np.arange(LANES)
    far = np.exp(-2j * np.pi * (row[:, None] * (4 * row[None, :] + 1) % (4 * blocks)) / (4 * blocks))
    near = np.exp(-2j * np.pi * (lane[:, None] * lane[None, :] % LANES) / LANES)
    turn = np.exp(-2j * np.pi * ((4 * row[:, None] + 1) * lane[None, :] % (4 * length)) / (4 * length))
    into = np.concatenate([far.T.real, far.T.imag], axis=0)
    back = np.concatenate([far.real, far.imag], axis=1) / length
    near_in = np.block([[near.real, near.imag], [-near.imag, near.real]])
    near_out = np.block([[near.real, -near.imag], [near.imag, near.real]])
    turn = np.stack([turn.real, turn.imag])
    as_short = lambda table: jnp.asarray(table.astype(np.float32)).astype(BF16)
    return {
        "into": as_short(into),
        "back": as_short(back),
        "near_in": as_short(near_in),
        "near_out": as_short(near_out),
        "turn": jnp.asarray(turn.astype(np.float32)),
    }


def times(real, imag, cos, sin):
    return real * cos - imag * sin, real * sin + imag * cos


def halves(value, axis):
    half = value.shape[axis] // 2
    return lax.slice_in_dim(value, 0, half, axis=axis), lax.slice_in_dim(value, half, 2 * half, axis=axis)


def conv_body(
    sig_ref,
    taps_ref,
    into_ref,
    near_in_ref,
    turn_ref,
    near_out_ref,
    back_ref,
    out_ref,
    both_ref,
    result_ref,
):
    groups, rows, lanes = sig_ref.shape
    blocks = into_ref.shape[1]
    per = groups * rows // blocks
    both_ref[0] = sig_ref[...].reshape(groups * rows, lanes).astype(F32)
    both_ref[1] = taps_ref[...].astype(F32)
    cos, sin = turn_ref[0], turn_ref[1]
    pairs = []
    for chan in range(per):
        at = pl.ds(chan, blocks, stride=per)
        both = jnp.concatenate([both_ref[0, at], both_ref[1, at]], axis=1).astype(BF16)
        far = jnp.dot(into_ref[...], both, preferred_element_type=F32)
        real, imag = halves(far, 0)
        pairs += [
            jnp.concatenate(times(r, i, cos, sin), axis=1)
            for r, i in zip(halves(real, 1), halves(imag, 1))
        ]
    pair = jnp.concatenate(pairs[::2] + pairs[1::2], axis=0).astype(BF16)
    points = halves(jnp.dot(pair, near_in_ref[...], preferred_element_type=F32), 0)
    product = times(*halves(points[0], 1), *halves(points[1], 1))
    pair = jnp.concatenate(product, axis=1).astype(BF16)
    near = jnp.dot(pair, near_out_ref[...], preferred_element_type=F32)
    for chan in range(per):
        real, imag = halves(near[chan * blocks : (chan + 1) * blocks], 1)
        pair = jnp.concatenate(times(real, imag, cos, -sin), axis=0).astype(BF16)
        at = pl.ds(chan, blocks, stride=per)
        result_ref[at] = jnp.dot(back_ref[...], pair, preferred_element_type=F32)
    out_ref[...] = result_ref[...].astype(BF16).reshape(groups, rows, lanes)


def pack_body(weight_hbm, out_w_hbm, taps_hbm, send_hbm, weight_ref, out_w_ref, taps_ref, send_ref, sems):
    copies = started([(taps_hbm, taps_ref), (weight_hbm, weight_ref), (out_w_hbm, out_w_ref)], sems)
    parts = weight_ref.shape[0]
    total, _, rows, lanes = send_ref.shape
    inner = out_w_ref.shape[1] // lanes
    ways = total // inner
    copies[0].wait()
    for s in range(inner):
        taps = taps_ref[:, s * lanes : (s + 1) * lanes].T.reshape(ways, rows, lanes).astype(BF16)
        for way in range(ways):
            send_ref[way * inner + s, parts + 1] = taps[way]
    finish(copies[1:])
    for s in range(inner):
        at = slice(s * lanes, (s + 1) * lanes)
        for way in range(ways):
            for part in range(parts):
                send_ref[way * inner + s, part] = weight_ref[part, :, at]
            send_ref[way * inner + s, parts] = out_w_ref[:, at]
    finish(started([(send_ref, send_hbm)], sems, len(copies)))


def repack_body(got_ref, send_ref, out_w_ref):
    sources, kinds, rows, lanes = got_ref.shape
    ways, tiles = send_ref.shape[0], send_ref.shape[1]
    parts = kinds - 2
    out_w_ref[...] = got_ref[:, parts]
    taps = got_ref[:, parts + 1].astype(F32)
    per = rows // ways
    for way in range(ways):
        for part in range(parts):
            send_ref[way, part * sources : (part + 1) * sources] = got_ref[:, part]
        piece = taps[:, way * per : (way + 1) * per].reshape(tiles - parts * sources, rows, lanes)
        send_ref[way, parts * sources :] = piece.astype(BF16)


def project_body(
    cores,
    place_ref,
    own_ref,
    other_hbm,
    halo_own_ref,
    halo_other_ref,
    gain_ref,
    taps_ref,
    skip_ref,
    got_ref,
    gates_ref,
    send_ref,
    filter_ref,
    other_ref,
    x_ref,
    proj_ref,
    sems,
):
    core = place_ref[0, 0]
    copies = started([(other_hbm, other_ref)], sems)
    parts = 3
    ways, _, rows, lanes = got_ref.shape
    groups = send_ref.shape[0]
    outer = groups // ways
    count, chans = gates_ref.shape[0], gates_ref.shape[1] // 2
    inner = count // lanes
    sources = outer * inner

    def column(part):
        pieces = [
            got_ref[x, part * sources + y * inner : part * sources + (y + 1) * inner].reshape(
                inner * rows, lanes
            )
            for y in range(outer)
            for x in range(ways)
        ]
        return jnp.concatenate(pieces, axis=0)

    first = parts * sources
    for y in range(outer):
        for x in range(ways):
            at = (y * ways + x) * rows
            filter_ref[at : at + rows] = got_ref[x, first + y]

    blocks, length, feats = own_ref.shape
    tp = x_ref.shape[1] // feats

    def put(pieces, at):
        total = sum(jnp.sum(piece * piece, axis=1, keepdims=True) for piece in pieces)
        scale = lax.rsqrt(total / (tp * feats) + 1e-05)
        for p, piece in enumerate(pieces):
            gain = gain_ref[:, p * feats : (p + 1) * feats]
            x_ref[at : at + piece.shape[0], p * feats : (p + 1) * feats] = (piece * scale * gain).astype(BF16)

    def project(count):
        got = jnp.dot(x_ref[:count], weight, preferred_element_type=F32)
        return got.astype(BF16).astype(F32)

    zs = blocks // tp
    weight = jnp.concatenate([column(part) for part in range(parts)], axis=1)
    last = core == cores - 1
    halo = [
        jnp.where(last, halo_own_ref[p].astype(F32), halo_other_ref[p].astype(F32)) for p in range(tp)
    ]
    for ref, at_core in ((own_ref, core), (other_ref, cores - 1 - core)):
        if ref is other_ref:
            finish(copies)
        for z in range(zs):
            put([ref[p * zs + z].astype(F32) for p in range(tp)], z * length)
        if ref is own_ref:
            put(halo, zs * length)
            got = project(zs * length + HALO)
            proj_ref[:HALO] = got[zs * length :]
        else:
            got = project(zs * length)
        for z in range(zs):
            at = pl.multiple_of(HALO + (z * cores + at_core) * length, HALO)
            proj_ref[pl.ds(at, length)] = got[z * length : (z + 1) * length]

    mine = pl.ds(pl.multiple_of(place_ref[0, 2] * chans, chans), chans)

    def tap(lag):
        return jnp.concatenate([taps_ref[lag, part : part + 1, mine] for part in range(parts)], axis=1)

    short = tap(0) * proj_ref[HALO:]
    for lag in range(1, taps_ref.shape[0]):
        short = short + tap(lag) * proj_ref[HALO - lag : HALO - lag + count]
    signal = short[:, chans : 2 * chans] * short[:, 2 * chans :]
    gates_ref[:, :chans] = short[:, :chans]
    gates_ref[:, chans:] = skip_ref[:, mine] * signal
    per = send_ref.shape[1] // inner
    pieces = [signal[b * lanes : (b + 1) * lanes].T.reshape(groups, per, lanes) for b in range(inner)]
    send_ref[...] = jnp.concatenate(pieces, axis=1).astype(BF16)


def tail_body(own_hbm, out_ref, sems):
    step = own_hbm.shape[0] // out_ref.shape[0]
    rows = pl.ds(own_hbm.shape[1] - HALO, HALO)
    finish(
        started([(own_hbm.at[step * p + step - 1, rows], out_ref.at[p]) for p in range(out_ref.shape[0])], sems)
    )


def gate_body(conv_ref, gates_ref, out_ref):
    groups, rows, lanes = conv_ref.shape
    inner = gates_ref.shape[0] // lanes
    per = rows // inner
    chans = groups * per
    conv = conv_ref[...].astype(F32)
    for b in range(inner):
        piece = conv[:, b * per : (b + 1) * per].reshape(chans, lanes).T
        at = slice(b * lanes, (b + 1) * lanes)
        gated = (gates_ref[at, :chans] * (piece + gates_ref[at, chans:])).astype(BF16)
        for p in range(out_ref.shape[1]):
            out_ref[b, p] = gated


def out_body(core_ref, gated_ref, own_ref, other_ref, out_ref):
    core = core_ref[0, 0]
    inner, tp, rows, chans = gated_ref.shape
    cores = other_ref.shape[0] // own_ref.shape[0] + 1
    zs = inner // cores
    ways = own_ref.shape[0] // zs
    x = jnp.concatenate([gated_ref[s, p] for p in range(tp) for s in range(inner)], axis=1)

    def column(ref, z):
        pieces = [ref[x * zs + z, y] for y in range(ref.shape[1]) for x in range(ways)]
        return jnp.concatenate(pieces, axis=0)

    weight = jnp.concatenate([column(ref, z) for ref in (own_ref, other_ref) for z in range(zs)], axis=1)
    out = jnp.dot(x, weight, preferred_element_type=F32).astype(BF16)
    for side, at_core in enumerate((core, cores - 1 - core)):
        for z in range(zs):
            k = side * zs + z
            at = pl.multiple_of((z * cores + at_core) * chans, chans)
            out_ref[:, pl.ds(at, chans)] = out[:, k * chans : (k + 1) * chans]


def shape(dims, dtype):
    return jax.ShapeDtypeStruct(dims, dtype)


def swap(value, axis):
    return lax.ppermute(value, axis, [(0, 1), (1, 0)])


def held(*arrays):
    return [pltpu.VMEM(array.shape, array.dtype) for array in arrays]


def copies_of(count):
    return [pltpu.SemaphoreType.DMA((count,))]


def shards(ways, tables, tokens, norm_gain, in_weight, short_taps, filter_response, skip_gain, out_weight):
    along, across = ways["y"], ways["x"]
    outer = along * across
    cores = ways["co"]
    inner = ways["zl"] * cores
    tp = ways["tp"]
    length, feats = tokens.shape
    chans = skip_gain.shape[0] // inner
    per = chans // outer
    depth, parts = in_weight.shape[0], in_weight.shape[1]
    rows = inner * per
    place = lax.axis_index(INNER)
    where = jnp.stack([lax.axis_index("co"), lax.axis_index("x"), place]).astype(jnp.int32).reshape(1, 3)

    with jax.named_scope("token_gather"):
        own = lax.all_gather(tokens, ("tp", "zl"), axis=0)
    with jax.named_scope("weight_gather"):
        kinds = parts + 2
        first = shape((along * inner, kinds, depth, LANES), BF16)
        weight = in_weight.transpose(1, 0, 2)
        send = call(
            pack_body,
            first,
            "hhhh",
            (weight, out_weight, filter_response),
            held(weight, out_weight, filter_response, first) + copies_of(4),
            limit=60,
        )
        got = lax.all_to_all(send, ("y",) + INNER, 0, 0)
        tiles = parts * along * inner + along
        piece_w = shape((along * inner, depth, LANES), BF16)
        send, piece = call(
            repack_body, (shape((across, tiles, depth, LANES), BF16), piece_w), "vvv", (got,)
        )
        got = lax.all_to_all(send, "x", 0, 0)
    with jax.named_scope("token_swap"):
        own, _ = lax.optimization_barrier((own, send))
        other = swap(own, "co")
        tail = call(
            tail_body,
            shape((tp, HALO, feats), BF16),
            "hv",
            (own,),
            copies_of(tp),
            limit=60,
            cost=pl.CostEstimate(flops=20000000000, bytes_accessed=2 * own.size, transcendentals=0),
        )
        halo_own = lax.ppermute(tail, OUTER, [(i, i + 1) for i in range(outer - 1)])
        halo_other = lax.ppermute(
            tail,
            OUTER + ("co",),
            [(i * cores + cores - 1, (i + 1) * cores) for i in range(outer - 1)],
        )
    with jax.named_scope("out_weight_gather"):
        out_w = lax.all_gather(piece.reshape(along, inner * depth, LANES), ("x", "zl"), axis=0)
    with jax.named_scope("project"):
        blocks = shape((outer, rows, LANES), BF16)
        wide = shape((ways["zl"] * length + HALO, tp * feats), BF16)
        proj = shape((HALO + inner * length, parts * chans), F32)
        gates, send, taps = call(
            functools.partial(project_body, cores),
            (
                shape((inner * length, 2 * chans), F32),
                blocks,
                shape((outer * rows, LANES), BF16),
            ),
            "svh" + "v" * 9,
            (where, own, other, halo_own, halo_other, norm_gain.reshape(1, tp * feats))
            + (short_taps, skip_gain.reshape(1, inner * chans), got),
            held(other, wide, proj) + copies_of(1),
        )
    with jax.named_scope("conv"):
        got = lax.all_to_all(send, OUTER, 0, 0)
        names = ("into", "near_in", "turn", "near_out", "back")
        operands = (got, taps) + tuple(tables[name] for name in names)
        count = outer * rows
        held_rows = [pltpu.VMEM((2, count, LANES), F32), pltpu.VMEM((count, LANES), F32)]
        conv = call(conv_body, blocks, "v" * (len(operands) + 1), operands, held_rows)
        conv = lax.all_to_all(conv, OUTER, 0, 0)
    with jax.named_scope("out_weight_swap"):
        other_w = swap(out_w, "co")
    with jax.named_scope("gate"):
        gated = call(gate_body, shape((inner, tp, length, chans), BF16), "vvv", (conv, gates))
        gated = lax.all_to_all(
            gated.reshape(inner * tp, length, chans), INNER + ("tp",), 0, 0
        ).reshape(inner, tp, length, chans)
    with jax.named_scope("out_project"):
        return call(
            out_body,
            shape((length, out_weight.shape[1]), BF16),
            "svvvv",
            (where[:, :1], gated, out_w, other_w),
        )


def solution(mesh):
    seq, tp = mesh.shape["seq"], mesh.shape["tp"]
    ways = {"y": seq // 16, "x": 4, "zl": 2, "co": 2, "tp": tp}
    fine = Mesh(mesh.devices.reshape(tuple(ways.values())), tuple(ways))
    placed = (
        P(SEQ, "tp"),
        P(),
        P(SEQ, None, "tp"),
        P(None, None, "tp"),
        P(SEQ, "tp"),
        P("tp"),
        P(SEQ, "tp"),
    )

    def run(*args):
        tables = transform_tables(args[0].shape[0])
        body = functools.partial(shards, ways, tables)
        return jax.shard_map(
            body, mesh=fine, in_specs=placed, out_specs=P(SEQ, "tp"), check_vma=False
        )(*args)

    return run
```

```python
import functools
import math

import jax
import jax.numpy as jnp
import numpy as np
from jax import lax
from jax.experimental import pallas as pl
from jax.experimental.pallas import tpu as pltpu
from jax.sharding import Mesh
from jax.sharding import PartitionSpec as P

F32 = jnp.float32
BF16 = jnp.bfloat16
LANES = 128
HALO = 16
MIB = 1024 * 1024
OUTER = ("y", "x")
INNER = ("zl", "co")
SEQ = OUTER + INNER


def call(body, out_shape, places, args, scratch=(), limit=16, cost=None):
    spaces = {"h": pltpu.HBM, "v": pltpu.VMEM, "s": pltpu.SMEM}
    specs = [pl.BlockSpec(memory_space=spaces[place]) for place in places]
    single = not isinstance(out_shape, tuple)
    outs = specs[len(args) :]
    return pl.pallas_call(
        body,
        out_shape=out_shape,
        in_specs=specs[: len(args)],
        out_specs=outs[0] if single else tuple(outs),
        scratch_shapes=scratch,
        cost_estimate=cost,
        compiler_params=pltpu.CompilerParams(vmem_limit_bytes=limit * MIB),
    )(*args)


def started(pairs, sems, first=0):
    copies = [
        pltpu.make_async_copy(source, target, sems.at[first + k])
        for k, (source, target) in enumerate(pairs)
    ]
    for copy in copies:
        copy.start()
    return copies


def finish(copies):
    for copy in copies:
        copy.wait()


def transform_tables(length):
    blocks = length // LANES
    row = np.arange(blocks)
    lane = np.arange(LANES)
    far = np.exp(-2j * np.pi * (row[:, None] * (4 * row[None, :] + 1) % (4 * blocks)) / (4 * blocks))
    near = np.exp(-2j * np.pi * (lane[:, None] * lane[None, :] % LANES) / LANES)
    turn = np.exp(-2j * np.pi * ((4 * row[:, None] + 1) * lane[None, :] % (4 * length)) / (4 * length))
    into = np.concatenate([far.T.real, far.T.imag], axis=0)
    back = np.concatenate([far.real, far.imag], axis=1) / length
    near_in = np.block([[near.real, near.imag], [-near.imag, near.real]])
    near_out = np.block([[near.real, -near.imag], [near.imag, near.real]])
    turn = np.stack([turn.real, turn.imag])
    as_short = lambda table: jnp.asarray(table.astype(np.float32)).astype(BF16)
    return {
        "into": as_short(into),
        "back": as_short(back),
        "near_in": as_short(near_in),
        "near_out": as_short(near_out),
        "turn": jnp.asarray(turn.astype(np.float32)),
    }


def times(real, imag, cos, sin):
    return real * cos - imag * sin, real * sin + imag * cos


def halves(value, axis):
    half = value.shape[axis] // 2
    return lax.slice_in_dim(value, 0, half, axis=axis), lax.slice_in_dim(value, half, 2 * half, axis=axis)


def conv_body(
    sig_ref,
    taps_ref,
    into_ref,
    near_in_ref,
    turn_ref,
    near_out_ref,
    back_ref,
    out_ref,
    both_ref,
    result_ref,
):
    groups, rows, lanes = sig_ref.shape
    blocks = into_ref.shape[1]
    per = groups * rows // blocks
    both_ref[0] = sig_ref[...].reshape(groups * rows, lanes).astype(F32)
    both_ref[1] = taps_ref[...].astype(F32)
    cos, sin = turn_ref[0], turn_ref[1]
    pairs = []
    for chan in range(per):
        at = pl.ds(chan, blocks, stride=per)
        both = jnp.concatenate([both_ref[0, at], both_ref[1, at]], axis=1).astype(BF16)
        far = jnp.dot(into_ref[...], both, preferred_element_type=F32)
        real, imag = halves(far, 0)
        pairs += [
            jnp.concatenate(times(r, i, cos, sin), axis=1)
            for r, i in zip(halves(real, 1), halves(imag, 1))
        ]
    pair = jnp.concatenate(pairs[::2] + pairs[1::2], axis=0).astype(BF16)
    points = halves(jnp.dot(pair, near_in_ref[...], preferred_element_type=F32), 0)
    product = times(*halves(points[0], 1), *halves(points[1], 1))
    pair = jnp.concatenate(product, axis=1).astype(BF16)
    near = jnp.dot(pair, near_out_ref[...], preferred_element_type=F32)
    for chan in range(per):
        real, imag = halves(near[chan * blocks : (chan + 1) * blocks], 1)
        pair = jnp.concatenate(times(real, imag, cos, -sin), axis=0).astype(BF16)
        at = pl.ds(chan, blocks, stride=per)
        result_ref[at] = jnp.dot(back_ref[...], pair, preferred_element_type=F32)
    out_ref[...] = result_ref[...].astype(BF16).reshape(groups, rows, lanes)


def pack_body(weight_hbm, out_w_hbm, taps_hbm, send_hbm, weight_ref, out_w_ref, taps_ref, send_ref, sems):
    copies = started([(taps_hbm, taps_ref), (weight_hbm, weight_ref), (out_w_hbm, out_w_ref)], sems)
    parts = weight_ref.shape[0]
    total, _, rows, lanes = send_ref.shape
    inner = out_w_ref.shape[1] // lanes
    ways = total // inner
    copies[0].wait()
    for s in range(inner):
        taps = taps_ref[:, s * lanes : (s + 1) * lanes].T.reshape(ways, rows, lanes).astype(BF16)
        for way in range(ways):
            send_ref[way * inner + s, parts + 1] = taps[way]
    finish(copies[1:])
    for s in range(inner):
        at = slice(s * lanes, (s + 1) * lanes)
        for way in range(ways):
            for part in range(parts):
                send_ref[way * inner + s, part] = weight_ref[part, :, at]
            send_ref[way * inner + s, parts] = out_w_ref[:, at]
    finish(started([(send_ref, send_hbm)], sems, len(copies)))


def repack_body(got_ref, send_ref, out_w_ref):
    sources, kinds, rows, lanes = got_ref.shape
    ways, tiles = send_ref.shape[0], send_ref.shape[1]
    parts = kinds - 2
    out_w_ref[...] = got_ref[:, parts]
    taps = got_ref[:, parts + 1].astype(F32)
    per = rows // ways
    for way in range(ways):
        for part in range(parts):
            send_ref[way, part * sources : (part + 1) * sources] = got_ref[:, part]
        piece = taps[:, way * per : (way + 1) * per].reshape(tiles - parts * sources, rows, lanes)
        send_ref[way, parts * sources :] = piece.astype(BF16)


def project_body(
    cores,
    place_ref,
    own_ref,
    other_hbm,
    halo_own_ref,
    halo_other_ref,
    gain_ref,
    taps_ref,
    skip_ref,
    got_ref,
    gates_ref,
    send_ref,
    filter_ref,
    other_ref,
    x_ref,
    proj_ref,
    sems,
):
    core = place_ref[0, 0]
    copies = started([(other_hbm, other_ref)], sems)
    parts = 3
    ways, _, rows, lanes = got_ref.shape
    groups = send_ref.shape[0]
    outer = groups // ways
    count, chans = gates_ref.shape[0], gates_ref.shape[1] // 2
    inner = count // lanes
    sources = outer * inner

    def column(part):
        pieces = [
            got_ref[x, part * sources + y * inner : part * sources + (y + 1) * inner].reshape(
                inner * rows, lanes
            )
            for y in range(outer)
            for x in range(ways)
        ]
        return jnp.concatenate(pieces, axis=0)

    first = parts * sources
    for y in range(outer):
        for x in range(ways):
            at = (y * ways + x) * rows
            filter_ref[at : at + rows] = got_ref[x, first + y]

    blocks, length, feats = own_ref.shape
    tp = x_ref.shape[1] // feats

    def put(pieces, at):
        total = sum(jnp.sum(piece * piece, axis=1, keepdims=True) for piece in pieces)
        scale = lax.rsqrt(total / (tp * feats) + 1e-05)
        for p, piece in enumerate(pieces):
            gain = gain_ref[:, p * feats : (p + 1) * feats]
            x_ref[at : at + piece.shape[0], p * feats : (p + 1) * feats] = (piece * scale * gain).astype(BF16)

    def project(count):
        got = jnp.dot(x_ref[:count], weight, preferred_element_type=F32)
        return got.astype(BF16).astype(F32)

    zs = blocks // tp
    weight = jnp.concatenate([column(part) for part in range(parts)], axis=1)
    last = core == cores - 1
    halo = [
        jnp.where(last, halo_own_ref[p].astype(F32), halo_other_ref[p].astype(F32)) for p in range(tp)
    ]
    for ref, at_core in ((own_ref, core), (other_ref, cores - 1 - core)):
        if ref is other_ref:
            finish(copies)
        for z in range(zs):
            put([ref[p * zs + z].astype(F32) for p in range(tp)], z * length)
        if ref is own_ref:
            put(halo, zs * length)
            got = project(zs * length + HALO)
            proj_ref[:HALO] = got[zs * length :]
        else:
            got = project(zs * length)
        for z in range(zs):
            at = pl.multiple_of(HALO + (z * cores + at_core) * length, HALO)
            proj_ref[pl.ds(at, length)] = got[z * length : (z + 1) * length]

    mine = pl.ds(pl.multiple_of(place_ref[0, 2] * chans, chans), chans)

    def tap(lag):
        return jnp.concatenate([taps_ref[lag, part : part + 1, mine] for part in range(parts)], axis=1)

    short = tap(0) * proj_ref[HALO:]
    for lag in range(1, taps_ref.shape[0]):
        short = short + tap(lag) * proj_ref[HALO - lag : HALO - lag + count]
    signal = short[:, chans : 2 * chans] * short[:, 2 * chans :]
    gates_ref[:, :chans] = short[:, :chans]
    gates_ref[:, chans:] = skip_ref[:, mine] * signal
    per = send_ref.shape[1] // inner
    pieces = [signal[b * lanes : (b + 1) * lanes].T.reshape(groups, per, lanes) for b in range(inner)]
    send_ref[...] = jnp.concatenate(pieces, axis=1).astype(BF16)


def tail_body(own_hbm, out_ref, sems):
    step = own_hbm.shape[0] // out_ref.shape[0]
    rows = pl.ds(own_hbm.shape[1] - HALO, HALO)
    finish(
        started([(own_hbm.at[step * p + step - 1, rows], out_ref.at[p]) for p in range(out_ref.shape[0])], sems)
    )


def gate_body(conv_ref, gates_ref, out_ref):
    groups, rows, lanes = conv_ref.shape
    inner = gates_ref.shape[0] // lanes
    per = rows // inner
    chans = groups * per
    conv = conv_ref[...].astype(F32)
    for b in range(inner):
        piece = conv[:, b * per : (b + 1) * per].reshape(chans, lanes).T
        at = slice(b * lanes, (b + 1) * lanes)
        gated = (gates_ref[at, :chans] * (piece + gates_ref[at, chans:])).astype(BF16)
        for p in range(out_ref.shape[1]):
            out_ref[b, p] = gated


def out_body(core_ref, gated_ref, own_ref, other_ref, out_ref):
    core = core_ref[0, 0]
    inner, tp, rows, chans = gated_ref.shape
    cores = other_ref.shape[0] // own_ref.shape[0] + 1
    zs = inner // cores
    ways = own_ref.shape[0] // zs
    x = jnp.concatenate([gated_ref[s, p] for p in range(tp) for s in range(inner)], axis=1)

    def column(ref, z):
        pieces = [ref[x * zs + z, y] for y in range(ref.shape[1]) for x in range(ways)]
        return jnp.concatenate(pieces, axis=0)

    weight = jnp.concatenate([column(ref, z) for ref in (own_ref, other_ref) for z in range(zs)], axis=1)
    out = jnp.dot(x, weight, preferred_element_type=F32).astype(BF16)
    for side, at_core in enumerate((core, cores - 1 - core)):
        for z in range(zs):
            k = side * zs + z
            at = pl.multiple_of((z * cores + at_core) * chans, chans)
            out_ref[:, pl.ds(at, chans)] = out[:, k * chans : (k + 1) * chans]


def shape(dims, dtype):
    return jax.ShapeDtypeStruct(dims, dtype)


def swap(value, axis):
    return lax.ppermute(value, axis, [(0, 1), (1, 0)])


def held(*arrays):
    return [pltpu.VMEM(array.shape, array.dtype) for array in arrays]


def copies_of(count):
    return [pltpu.SemaphoreType.DMA((count,))]


def shards(ways, tables, tokens, norm_gain, in_weight, short_taps, filter_response, skip_gain, out_weight):
    along, across = ways["y"], ways["x"]
    outer = along * across
    cores = ways["co"]
    inner = ways["zl"] * cores
    tp = ways["tp"]
    length, feats = tokens.shape
    chans = skip_gain.shape[0] // inner
    per = chans // outer
    depth, parts = in_weight.shape[0], in_weight.shape[1]
    rows = inner * per
    place = lax.axis_index(INNER)
    where = jnp.stack([lax.axis_index("co"), lax.axis_index("x"), place]).astype(jnp.int32).reshape(1, 3)

    with jax.named_scope("token_gather"):
        own = lax.all_gather(tokens, ("tp", "zl"), axis=0)
    with jax.named_scope("weight_gather"):
        kinds = parts + 2
        first = shape((along * inner, kinds, depth, LANES), BF16)
        weight = in_weight.transpose(1, 0, 2)
        send = call(
            pack_body,
            first,
            "hhhh",
            (weight, out_weight, filter_response),
            held(weight, out_weight, filter_response, first) + copies_of(4),
            limit=60,
        )
        got = lax.all_to_all(send, ("y",) + INNER, 0, 0)
        tiles = parts * along * inner + along
        piece_w = shape((along * inner, depth, LANES), BF16)
        send, piece = call(
            repack_body, (shape((across, tiles, depth, LANES), BF16), piece_w), "vvv", (got,)
        )
        got = lax.all_to_all(send, "x", 0, 0)
    with jax.named_scope("token_swap"):
        own, _ = lax.optimization_barrier((own, send))
        other = swap(own, "co")
        tail = call(
            tail_body,
            shape((tp, HALO, feats), BF16),
            "hv",
            (pltpu.with_memory_space_constraint(own, pltpu.HBM),),
            copies_of(tp),
            cost=pl.CostEstimate(flops=20000000000, bytes_accessed=2 * own.size, transcendentals=0),
        )
        halo_own = lax.ppermute(tail, OUTER, [(i, i + 1) for i in range(outer - 1)])
        halo_other = lax.ppermute(
            tail,
            OUTER + ("co",),
            [(i * cores + cores - 1, (i + 1) * cores) for i in range(outer - 1)],
        )
    with jax.named_scope("out_weight_gather"):
        out_w = lax.all_gather(piece.reshape(along, inner * depth, LANES), ("x", "zl"), axis=0)
    with jax.named_scope("project"):
        blocks = shape((outer, rows, LANES), BF16)
        wide = shape((ways["zl"] * length + HALO, tp * feats), BF16)
        proj = shape((HALO + inner * length, parts * chans), F32)
        gates, send, taps = call(
            functools.partial(project_body, cores),
            (
                shape((inner * length, 2 * chans), F32),
                blocks,
                shape((outer * rows, LANES), BF16),
            ),
            "svh" + "v" * 9,
            (where, own, other, halo_own, halo_other, norm_gain.reshape(1, tp * feats))
            + (short_taps, skip_gain.reshape(1, inner * chans), got),
            held(other, wide, proj) + copies_of(1),
        )
    with jax.named_scope("conv"):
        got = lax.all_to_all(send, OUTER, 0, 0)
        names = ("into", "near_in", "turn", "near_out", "back")
        operands = (got, taps) + tuple(tables[name] for name in names)
        count = outer * rows
        held_rows = [pltpu.VMEM((2, count, LANES), F32), pltpu.VMEM((count, LANES), F32)]
        conv = call(conv_body, blocks, "v" * (len(operands) + 1), operands, held_rows)
        conv = lax.all_to_all(conv, OUTER, 0, 0)
    with jax.named_scope("out_weight_swap"):
        other_w = swap(out_w, "co")
    with jax.named_scope("gate"):
        gated = call(gate_body, shape((inner, tp, length, chans), BF16), "vvv", (conv, gates))
        gated = lax.all_to_all(
            gated.reshape(inner * tp, length, chans), INNER + ("tp",), 0, 0
        ).reshape(inner, tp, length, chans)
    with jax.named_scope("out_project"):
        return call(
            out_body,
            shape((length, out_weight.shape[1]), BF16),
            "svvvv",
            (where[:, :1], gated, out_w, other_w),
        )


def solution(mesh):
    seq, tp = mesh.shape["seq"], mesh.shape["tp"]
    ways = {"y": seq // 16, "x": 4, "zl": 2, "co": 2, "tp": tp}
    fine = Mesh(mesh.devices.reshape(tuple(ways.values())), tuple(ways))
    placed = (
        P(SEQ, "tp"),
        P(),
        P(SEQ, None, "tp"),
        P(None, None, "tp"),
        P(SEQ, "tp"),
        P("tp"),
        P(SEQ, "tp"),
    )

    def run(*args):
        tables = transform_tables(args[0].shape[0])
        body = functools.partial(shards, ways, tables)
        return jax.shard_map(
            body, mesh=fine, in_specs=placed, out_specs=P(SEQ, "tp"), check_vma=False
        )(*args)

    return run
```

```python
import functools
import math

import jax
import jax.numpy as jnp
import numpy as np
from jax import lax
from jax.experimental import pallas as pl
from jax.experimental.pallas import tpu as pltpu
from jax.sharding import Mesh
from jax.sharding import PartitionSpec as P

F32 = jnp.float32
BF16 = jnp.bfloat16
LANES = 128
HALO = 16
MIB = 1024 * 1024
OUTER = ("y", "x")
INNER = ("zl", "co")
SEQ = OUTER + INNER


def call(body, out_shape, places, args, scratch=(), limit=16, cost=None):
    spaces = {"h": pltpu.HBM, "v": pltpu.VMEM, "s": pltpu.SMEM}
    specs = [pl.BlockSpec(memory_space=spaces[place]) for place in places]
    single = not isinstance(out_shape, tuple)
    outs = specs[len(args) :]
    return pl.pallas_call(
        body,
        out_shape=out_shape,
        in_specs=specs[: len(args)],
        out_specs=outs[0] if single else tuple(outs),
        scratch_shapes=scratch,
        cost_estimate=cost,
        compiler_params=pltpu.CompilerParams(vmem_limit_bytes=limit * MIB),
    )(*args)


def started(pairs, sems, first=0):
    copies = [
        pltpu.make_async_copy(source, target, sems.at[first + k])
        for k, (source, target) in enumerate(pairs)
    ]
    for copy in copies:
        copy.start()
    return copies


def finish(copies):
    for copy in copies:
        copy.wait()


def transform_tables(length):
    blocks = length // LANES
    row = np.arange(blocks)
    lane = np.arange(LANES)
    far = np.exp(-2j * np.pi * (row[:, None] * (4 * row[None, :] + 1) % (4 * blocks)) / (4 * blocks))
    near = np.exp(-2j * np.pi * (lane[:, None] * lane[None, :] % LANES) / LANES)
    turn = np.exp(-2j * np.pi * ((4 * row[:, None] + 1) * lane[None, :] % (4 * length)) / (4 * length))
    into = np.concatenate([far.T.real, far.T.imag], axis=0)
    back = np.concatenate([far.real, far.imag], axis=1) / length
    near_in = np.block([[near.real, near.imag], [-near.imag, near.real]])
    near_out = np.block([[near.real, -near.imag], [near.imag, near.real]])
    turn = np.stack([turn.real, turn.imag])
    as_short = lambda table: jnp.asarray(table.astype(np.float32)).astype(BF16)
    return {
        "into": as_short(into),
        "back": as_short(back),
        "near_in": as_short(near_in),
        "near_out": as_short(near_out),
        "turn": jnp.asarray(turn.astype(np.float32)),
    }


def times(real, imag, cos, sin):
    return real * cos - imag * sin, real * sin + imag * cos


def halves(value, axis):
    half = value.shape[axis] // 2
    return lax.slice_in_dim(value, 0, half, axis=axis), lax.slice_in_dim(value, half, 2 * half, axis=axis)


def conv_body(
    sig_ref,
    taps_ref,
    into_ref,
    near_in_ref,
    turn_ref,
    near_out_ref,
    back_ref,
    out_ref,
    both_ref,
    result_ref,
):
    groups, rows, lanes = sig_ref.shape
    blocks = into_ref.shape[1]
    per = groups * rows // blocks
    both_ref[0] = sig_ref[...].reshape(groups * rows, lanes).astype(F32)
    both_ref[1] = taps_ref[...].astype(F32)
    cos, sin = turn_ref[0], turn_ref[1]
    pairs = []
    for chan in range(per):
        at = pl.ds(chan, blocks, stride=per)
        both = jnp.concatenate([both_ref[0, at], both_ref[1, at]], axis=1).astype(BF16)
        far = jnp.dot(into_ref[...], both, preferred_element_type=F32)
        real, imag = halves(far, 0)
        pairs += [
            jnp.concatenate(times(r, i, cos, sin), axis=1)
            for r, i in zip(halves(real, 1), halves(imag, 1))
        ]
    pair = jnp.concatenate(pairs[::2] + pairs[1::2], axis=0).astype(BF16)
    points = halves(jnp.dot(pair, near_in_ref[...], preferred_element_type=F32), 0)
    product = times(*halves(points[0], 1), *halves(points[1], 1))
    pair = jnp.concatenate(product, axis=1).astype(BF16)
    near = jnp.dot(pair, near_out_ref[...], preferred_element_type=F32)
    for chan in range(per):
        real, imag = halves(near[chan * blocks : (chan + 1) * blocks], 1)
        pair = jnp.concatenate(times(real, imag, cos, -sin), axis=0).astype(BF16)
        at = pl.ds(chan, blocks, stride=per)
        result_ref[at] = jnp.dot(back_ref[...], pair, preferred_element_type=F32)
    out_ref[...] = result_ref[...].astype(BF16).reshape(groups, rows, lanes)


def pack_body(weight_hbm, out_w_hbm, taps_hbm, send_hbm, weight_ref, out_w_ref, taps_ref, send_ref, sems):
    copies = started([(taps_hbm, taps_ref), (weight_hbm, weight_ref), (out_w_hbm, out_w_ref)], sems)
    parts = weight_ref.shape[0]
    total, _, rows, lanes = send_ref.shape
    inner = out_w_ref.shape[1] // lanes
    ways = total // inner
    copies[0].wait()
    for s in range(inner):
        taps = taps_ref[:, s * lanes : (s + 1) * lanes].T.reshape(ways, rows, lanes).astype(BF16)
        for way in range(ways):
            send_ref[way * inner + s, parts + 1] = taps[way]
    finish(copies[1:])
    for s in range(inner):
        at = slice(s * lanes, (s + 1) * lanes)
        for way in range(ways):
            for part in range(parts):
                send_ref[way * inner + s, part] = weight_ref[part, :, at]
            send_ref[way * inner + s, parts] = out_w_ref[:, at]
    finish(started([(send_ref, send_hbm)], sems, len(copies)))


def repack_body(got_ref, send_ref, out_w_ref):
    sources, kinds, rows, lanes = got_ref.shape
    ways, tiles = send_ref.shape[0], send_ref.shape[1]
    parts = kinds - 2
    out_w_ref[...] = got_ref[:, parts]
    taps = got_ref[:, parts + 1].astype(F32)
    per = rows // ways
    for way in range(ways):
        for part in range(parts):
            send_ref[way, part * sources : (part + 1) * sources] = got_ref[:, part]
        piece = taps[:, way * per : (way + 1) * per].reshape(tiles - parts * sources, rows, lanes)
        send_ref[way, parts * sources :] = piece.astype(BF16)


def scaled(pieces, gain_ref):
    feats = pieces[0].shape[1]
    total = sum(jnp.sum(piece * piece, axis=1, keepdims=True) for piece in pieces)
    scale = lax.rsqrt(total / gain_ref.shape[1] + 1e-05)
    return [
        (piece * scale * gain_ref[:, p * feats : (p + 1) * feats]).astype(BF16)
        for p, piece in enumerate(pieces)
    ]


def norm_body(tok_ref, gain_ref, out_ref):
    zs, length = out_ref.shape[:2]
    feats = tok_ref.shape[2]
    tp = tok_ref.shape[0] // zs
    for z in range(zs):
        pieces = [tok_ref[p * zs + z].astype(F32) for p in range(tp)]
        for p, piece in enumerate(scaled(pieces, gain_ref)):
            out_ref[z, :, p * feats : (p + 1) * feats] = piece


def project_body(
    cores,
    place_ref,
    own_ref,
    other_ref,
    halo_own_ref,
    halo_other_ref,
    gain_ref,
    taps_ref,
    skip_ref,
    got_ref,
    gates_ref,
    send_ref,
    filter_ref,
    x_ref,
    proj_ref,
):
    core = place_ref[0, 0]
    parts = 3
    ways, _, rows, lanes = got_ref.shape
    groups = send_ref.shape[0]
    outer = groups // ways
    count, chans = gates_ref.shape[0], gates_ref.shape[1] // 2
    inner = count // lanes
    sources = outer * inner

    def column(part):
        pieces = [
            got_ref[x, part * sources + y * inner : part * sources + (y + 1) * inner].reshape(
                inner * rows, lanes
            )
            for y in range(outer)
            for x in range(ways)
        ]
        return jnp.concatenate(pieces, axis=0)

    first = parts * sources
    for y in range(outer):
        for x in range(ways):
            at = (y * ways + x) * rows
            filter_ref[at : at + rows] = got_ref[x, first + y]

    zs, length = own_ref.shape[:2]
    tp, _, feats = halo_own_ref.shape

    def project(count):
        got = jnp.dot(x_ref[:count], weight, preferred_element_type=F32)
        return got.astype(BF16).astype(F32)

    weight = jnp.concatenate([column(part) for part in range(parts)], axis=1)
    last = core == cores - 1
    halo = [
        jnp.where(last, halo_own_ref[p].astype(F32), halo_other_ref[p].astype(F32)) for p in range(tp)
    ]
    for ref, at_core in ((own_ref, core), (other_ref, cores - 1 - core)):
        for z in range(zs):
            x_ref[z * length : (z + 1) * length] = ref[z]
        if ref is own_ref:
            for p, piece in enumerate(scaled(halo, gain_ref)):
                x_ref[zs * length :, p * feats : (p + 1) * feats] = piece
            got = project(zs * length + HALO)
            proj_ref[:HALO] = got[zs * length :]
        else:
            got = project(zs * length)
        for z in range(zs):
            at = pl.multiple_of(HALO + (z * cores + at_core) * length, HALO)
            proj_ref[pl.ds(at, length)] = got[z * length : (z + 1) * length]

    mine = pl.ds(pl.multiple_of(place_ref[0, 2] * chans, chans), chans)

    def tap(lag):
        return jnp.concatenate([taps_ref[lag, part : part + 1, mine] for part in range(parts)], axis=1)

    short = tap(0) * proj_ref[HALO:]
    for lag in range(1, taps_ref.shape[0]):
        short = short + tap(lag) * proj_ref[HALO - lag : HALO - lag + count]
    signal = short[:, chans : 2 * chans] * short[:, 2 * chans :]
    gates_ref[:, :chans] = short[:, :chans]
    gates_ref[:, chans:] = skip_ref[:, mine] * signal
    per = send_ref.shape[1] // inner
    pieces = [signal[b * lanes : (b + 1) * lanes].T.reshape(groups, per, lanes) for b in range(inner)]
    send_ref[...] = jnp.concatenate(pieces, axis=1).astype(BF16)


def tail_body(own_hbm, out_ref, sems):
    step = own_hbm.shape[0] // out_ref.shape[0]
    rows = pl.ds(own_hbm.shape[1] - HALO, HALO)
    finish(
        started([(own_hbm.at[step * p + step - 1, rows], out_ref.at[p]) for p in range(out_ref.shape[0])], sems)
    )


def gate_body(conv_ref, gates_ref, out_ref):
    groups, rows, lanes = conv_ref.shape
    inner = gates_ref.shape[0] // lanes
    per = rows // inner
    chans = groups * per
    conv = conv_ref[...].astype(F32)
    for b in range(inner):
        piece = conv[:, b * per : (b + 1) * per].reshape(chans, lanes).T
        at = slice(b * lanes, (b + 1) * lanes)
        gated = (gates_ref[at, :chans] * (piece + gates_ref[at, chans:])).astype(BF16)
        for p in range(out_ref.shape[1]):
            out_ref[b, p] = gated


def out_body(core_ref, gated_ref, own_ref, other_ref, out_ref):
    core = core_ref[0, 0]
    inner, tp, rows, chans = gated_ref.shape
    cores = other_ref.shape[0] // own_ref.shape[0] + 1
    zs = inner // cores
    ways = own_ref.shape[0] // zs
    x = jnp.concatenate([gated_ref[s, p] for p in range(tp) for s in range(inner)], axis=1)

    def column(ref, z):
        pieces = [ref[x * zs + z, y] for y in range(ref.shape[1]) for x in range(ways)]
        return jnp.concatenate(pieces, axis=0)

    weight = jnp.concatenate([column(ref, z) for ref in (own_ref, other_ref) for z in range(zs)], axis=1)
    out = jnp.dot(x, weight, preferred_element_type=F32).astype(BF16)
    for side, at_core in enumerate((core, cores - 1 - core)):
        for z in range(zs):
            k = side * zs + z
            at = pl.multiple_of((z * cores + at_core) * chans, chans)
            out_ref[:, pl.ds(at, chans)] = out[:, k * chans : (k + 1) * chans]


def shape(dims, dtype):
    return jax.ShapeDtypeStruct(dims, dtype)


def swap(value, axis):
    return lax.ppermute(value, axis, [(0, 1), (1, 0)])


def held(*arrays):
    return [pltpu.VMEM(array.shape, array.dtype) for array in arrays]


def copies_of(count):
    return [pltpu.SemaphoreType.DMA((count,))]


def shards(ways, tables, tokens, norm_gain, in_weight, short_taps, filter_response, skip_gain, out_weight):
    along, across = ways["y"], ways["x"]
    outer = along * across
    cores = ways["co"]
    inner = ways["zl"] * cores
    tp = ways["tp"]
    length, feats = tokens.shape
    chans = skip_gain.shape[0] // inner
    per = chans // outer
    depth, parts = in_weight.shape[0], in_weight.shape[1]
    rows = inner * per
    place = lax.axis_index(INNER)
    where = jnp.stack([lax.axis_index("co"), lax.axis_index("x"), place]).astype(jnp.int32).reshape(1, 3)

    with jax.named_scope("token_gather"):
        own = lax.all_gather(tokens, ("tp", "zl"), axis=0)
    with jax.named_scope("weight_gather"):
        kinds = parts + 2
        first = shape((along * inner, kinds, depth, LANES), BF16)
        weight = in_weight.transpose(1, 0, 2)
        send = call(
            pack_body,
            first,
            "hhhh",
            (weight, out_weight, filter_response),
            held(weight, out_weight, filter_response, first) + copies_of(4),
            limit=60,
        )
        got = lax.all_to_all(send, ("y",) + INNER, 0, 0)
        tiles = parts * along * inner + along
        piece_w = shape((along * inner, depth, LANES), BF16)
        send, piece = call(
            repack_body, (shape((across, tiles, depth, LANES), BF16), piece_w), "vvv", (got,)
        )
        got = lax.all_to_all(send, "x", 0, 0)
    with jax.named_scope("token_swap"):
        own, _ = lax.optimization_barrier((own, send))
        other = swap(own, "co")
        tail = call(
            tail_body,
            shape((tp, HALO, feats), BF16),
            "hv",
            (pltpu.with_memory_space_constraint(own, pltpu.HBM),),
            copies_of(tp),
            cost=pl.CostEstimate(flops=20000000000, bytes_accessed=2 * own.size, transcendentals=0),
        )
        halo_own = lax.ppermute(tail, OUTER, [(i, i + 1) for i in range(outer - 1)])
        halo_other = lax.ppermute(
            tail,
            OUTER + ("co",),
            [(i * cores + cores - 1, (i + 1) * cores) for i in range(outer - 1)],
        )
        gain = norm_gain.reshape(1, tp * feats)
        normed = shape((ways["zl"], length, tp * feats), BF16)
        x_own = call(norm_body, normed, "vvv", (own, gain))
        x_other = call(norm_body, normed, "vvv", (other, gain))
    with jax.named_scope("out_weight_gather"):
        out_w = lax.all_gather(piece.reshape(along, inner * depth, LANES), ("x", "zl"), axis=0)
    with jax.named_scope("project"):
        blocks = shape((outer, rows, LANES), BF16)
        wide = shape((ways["zl"] * length + HALO, tp * feats), BF16)
        proj = shape((HALO + inner * length, parts * chans), F32)
        gates, send, taps = call(
            functools.partial(project_body, cores),
            (
                shape((inner * length, 2 * chans), F32),
                blocks,
                shape((outer * rows, LANES), BF16),
            ),
            "s" + "v" * 11,
            (where, x_own, x_other, halo_own, halo_other, gain)
            + (short_taps, skip_gain.reshape(1, inner * chans), got),
            held(wide, proj),
        )
    with jax.named_scope("conv"):
        got = lax.all_to_all(send, OUTER, 0, 0)
        names = ("into", "near_in", "turn", "near_out", "back")
        operands = (got, taps) + tuple(tables[name] for name in names)
        count = outer * rows
        held_rows = [pltpu.VMEM((2, count, LANES), F32), pltpu.VMEM((count, LANES), F32)]
        conv = call(conv_body, blocks, "v" * (len(operands) + 1), operands, held_rows)
        conv = lax.all_to_all(conv, OUTER, 0, 0)
    with jax.named_scope("out_weight_swap"):
        other_w = swap(out_w, "co")
    with jax.named_scope("gate"):
        gated = call(gate_body, shape((inner, tp, length, chans), BF16), "vvv", (conv, gates))
        gated = lax.all_to_all(
            gated.reshape(inner * tp, length, chans), INNER + ("tp",), 0, 0
        ).reshape(inner, tp, length, chans)
    with jax.named_scope("out_project"):
        return call(
            out_body,
            shape((length, out_weight.shape[1]), BF16),
            "svvvv",
            (where[:, :1], gated, out_w, other_w),
        )


def solution(mesh):
    seq, tp = mesh.shape["seq"], mesh.shape["tp"]
    ways = {"y": seq // 16, "x": 4, "zl": 2, "co": 2, "tp": tp}
    fine = Mesh(mesh.devices.reshape(tuple(ways.values())), tuple(ways))
    placed = (
        P(SEQ, "tp"),
        P(),
        P(SEQ, None, "tp"),
        P(None, None, "tp"),
        P(SEQ, "tp"),
        P("tp"),
        P(SEQ, "tp"),
    )

    def run(*args):
        tables = transform_tables(args[0].shape[0])
        body = functools.partial(shards, ways, tables)
        return jax.shard_map(
            body, mesh=fine, in_specs=placed, out_specs=P(SEQ, "tp"), check_vma=False
        )(*args)

    return run
```
